32 devices in a mesh: grp: 4 (over y, x), mem: 8 (over z, core).
Axes of the slice: x: 2, y: 2, z: 4, core: 2. Of those that a mesh axis runs over, the one named last changes fastest.
Arguments:
- images: bfloat16 [1024, 18432], P(('grp', 'mem')), may hold values from -24 to 24
- classes: int32 [1024], P(('grp', 'mem')), may hold values from 0 to 199, as said below
- rotations: int32 [1024], P(('grp', 'mem')), may hold values from 0 to 35
- bins: int32 [1024], P(('grp', 'mem')), may hold values from 0 to 15
- ctf_table: float32 [16, 18432], replicated, may hold values from -1 to 1
Outputs:
- averages: float32 [200, 18432], P('grp', 'mem')
The draws below stay inside these ranges and needn't reach their ends.
Inputs may be any that keep to these rules, and one draw needn't show every extreme that they name: The owner of a class c is c // 50. In each aligned block of 32 particles (one device's), at most 16 particles belong to classes of one owner, and exactly 16 do for some owner in every block.
All inputs are finite; a program needn't handle non-finite values.
Results may differ from the reference program's by a relative error of at most 0.0003.
Values may be sent and summed in bfloat16 or wider, within the bound.
No kernel may reach another device: no remote copies, remote signals or barrier semaphores. Data moves between devices by JAX's collectives and lax.ppermute only.
A program may use at most 256 MiB of HBM per device.

```python
import jax
import jax.numpy as jnp
from jax import lax

ANGLES = 144
ROTS = 36
BINS = 16
CPG = 50
TOK_DEV = 32
SHIFT = 4
F = 18432
CLASSES = 200
PARTICLES = 1024
N_GRP = 4


def draw_classes(key, part):
    blocks = PARTICLES // TOK_DEV
    half = TOK_DEV // 2
    order = jax.random.permutation(jax.random.fold_in(key, 7), CPG)

    def one_block(block_key):
        keys = jax.random.split(block_key, 5)
        full = jax.random.randint(keys[0], (), 0, N_GRP)
        others = jax.random.randint(keys[1], (TOK_DEV - half,), 0, N_GRP - 1)
        others = others + (others >= full).astype(jnp.int32)
        owners = jnp.concatenate([jnp.full((half,), full, jnp.int32), others.astype(jnp.int32)])
        owners = owners[jax.random.permutation(keys[2], TOK_DEV)]
        first = jax.random.randint(keys[3], (TOK_DEV,), 0, CPG)
        second = jax.random.randint(keys[4], (TOK_DEV,), 0, CPG)
        local = order[jnp.minimum(first, second)]
        return (owners * CPG + local).astype(jnp.int32)
    block_keys = jax.random.split(jax.random.fold_in(key, 11), blocks)
    return jax.vmap(one_block)(block_keys).reshape(-1)


def with_ends(array, stream_key, smallest, high):
    longest = array.shape.index(max(array.shape))
    spots = []
    for shift in (0, 1):
        where = [jax.random.randint(jax.random.fold_in(stream_key, axis), (), 0, length) for axis, length in enumerate(array.shape)]
        where[longest] = (where[longest] + shift) % array.shape[longest]
        spots.append(tuple(where))
    return array.at[spots[0]].set(smallest).at[spots[1]].set(high)


def block_scale(own_key, shape, cuts, smallest, high):
    factor_of, own = 1.0, jax.random.fold_in(own_key, 6)
    for position, parts in cuts:
        draws = jnp.exp(jax.random.uniform(jax.random.fold_in(own, position), (parts,), jnp.float32, smallest / len(cuts), high / len(cuts)))
        factor_of = factor_of * jnp.repeat(draws, shape[position] // parts).reshape([-1 if axis == position else 1 for axis in range(len(shape))])
    return factor_of


def bell_draw(key, dims, deviation, most, cuts=(), held_as=jnp.bfloat16):
    drawn = jax.random.normal(key, dims, jnp.float32) * deviation
    if len(cuts) > 0:
        drawn = block_scale(key, dims, cuts, -0.22, 0.18) * drawn
    return jnp.clip(drawn, min=-most, max=most).astype(held_as)


def setup_inputs(seed: int = 0) -> dict:
    splits = jax.random.split(jax.random.key(seed), 6)
    images = bell_draw(splits[0], (PARTICLES, F), 4.0, 24.0, ((0, 32),))
    classes = draw_classes(jax.random.fold_in(splits[5], 71), 0)
    rotations = with_ends(jax.random.randint(splits[2], (PARTICLES,), 0, ROTS), jax.random.fold_in(splits[2], 1), 0, ROTS - 1).astype(jnp.int32)
    bins = with_ends(jax.random.randint(splits[3], (PARTICLES,), 0, BINS), jax.random.fold_in(splits[3], 1), 0, BINS - 1).astype(jnp.int32)
    ctf_table = jnp.clip(jax.random.uniform(splits[4], (BINS, F), jnp.float32, -1.0, 1.0), -1.0, 1.0)
    return {"images": images, "classes": classes, "rotations": rotations, "bins": bins, "ctf_table": ctf_table}


wiener_term = 1.0


def rotate(values, turns):
    count = values.shape[0]
    shaped = values.reshape(count, -1, ANGLES)
    source = (jnp.arange(ANGLES, dtype=jnp.int32)[None, :] + SHIFT * turns[:, None]) % ANGLES
    moved = jnp.take_along_axis(shaped, source[:, None, :].astype(jnp.int32), axis=2)
    return moved.reshape(count, -1)


def reference(images, classes, rotations, bins, ctf_table):
    blocks = images.shape[0] // TOK_DEV
    stack = (images.reshape(blocks, TOK_DEV, -1), classes.reshape(blocks, TOK_DEV),
             rotations.reshape(blocks, TOK_DEV), bins.reshape(blocks, TOK_DEV))

    def step(carry, pieces):
        numer, denom = carry
        block_images, block_classes, block_turns, block_bins = pieces
        ctf_rows = ctf_table[block_bins]
        aligned = rotate(ctf_rows * block_images.astype(jnp.float32), block_turns)
        weights = rotate(ctf_rows * ctf_rows, block_turns)
        numer = numer + jax.ops.segment_sum(aligned, block_classes, CLASSES)
        denom = denom + jax.ops.segment_sum(weights, block_classes, CLASSES)
        return (numer, denom), None

    start = (jnp.zeros((CLASSES, F), jnp.float32), jnp.zeros((CLASSES, F), jnp.float32))
    (numer, denom), _ = lax.scan(step, start, stack)
    return numer / (denom + wiener_term)
```

```python
import functools

import jax
import jax.numpy as jnp
from jax import lax
from jax.experimental import pallas as pl
from jax.experimental.pallas import tpu as pltpu
from jax.sharding import PartitionSpec as P

ANGLES = 144
ROTS = 36
BINS = 16
CPG = 50
SHIFT = 4

LANES = 128
ROWS = 8
CPAD = -(-CPG // ROWS) * ROWS
PIECES = 3
PAIRS = -(-ROTS * BINS // LANES) * LANES
LEVELS = max(ROTS - 1, 1).bit_length()
VMEM_LIMIT = 56 * 1024 * 1024

wiener_term = 1.0

F32 = jnp.float32
BF16 = jnp.bfloat16
NT = (((1,), (1,)), ((), ()))
ANY = pl.BlockSpec(memory_space=pl.ANY)
VMEM = pl.BlockSpec(memory_space=pltpu.VMEM)


def partner(index, step, size):
    if size & (size - 1) == 0:
        return index ^ step
    return (index + step) % size


def send(value, axis, step):
    size = lax.axis_size(axis)
    return lax.ppermute(value, axis, [(i, partner(i, step, size)) for i in range(size)])


def identity():
    rows = lax.broadcasted_iota(jnp.int32, (LANES, LANES), 0)
    cols = lax.broadcasted_iota(jnp.int32, (LANES, LANES), 1)
    return (rows == cols).astype(BF16)


def turned(block, amount):
    amount %= ANGLES
    if amount == 0:
        return block
    if amount % ROWS == 0:
        return jnp.concatenate([block[amount:], block[:amount]], axis=0)
    return pltpu.roll(block, ANGLES - amount, 0)


def split(value):
    high = value.astype(BF16)
    low = (value - high.astype(F32)).astype(BF16)
    return high, low


def params(flops, moved):
    return dict(
        compiler_params=pltpu.CompilerParams(vmem_limit_bytes=VMEM_LIMIT),
        cost_estimate=pl.CostEstimate(flops=flops, bytes_accessed=moved, transcendentals=0),
    )


def pack_kernel(mem, cols, edges, img, cls, rot, bns, own_tag, *rest):
    size = mem
    count = cls.shape[1]
    groups = count // ROWS
    chunks = len(edges) - 1
    msgs = rest[: chunks * (size - 1)]
    tagbuf, sems, tag_sems = rest[chunks * (size - 1) :]
    me = lax.axis_index("mem")
    copies = []
    for chunk in range(chunks):
        width = (edges[chunk + 1] - edges[chunk]) * LANES
        for step in range(1, size):
            dest = partner(me, step, size)
            start = pl.multiple_of(dest * cols + edges[chunk] * LANES, LANES)
            out = msgs[chunk * (size - 1) + step - 1]
            for g in range(groups):
                copies.append(
                    pltpu.make_async_copy(
                        img.at[pl.ds(g * ROWS, ROWS), pl.ds(start, width)],
                        out.at[:, pl.ds(g * width, width)],
                        sems.at[len(copies)],
                    )
                )
                copies[-1].start()
    label = cls[...]
    owner = jnp.zeros_like(label)
    for g in range(1, lax.axis_size("grp")):
        owner += (label >= g * CPG).astype(jnp.int32)
    row = lax.broadcasted_iota(jnp.int32, (ROWS, count), 0)
    stack = jnp.where(
        row == 0,
        owner,
        jnp.where(
            row == 1,
            label - owner * CPG,
            jnp.where(row == 2, bns[...], jnp.where(row == 3, rot[...], 0)),
        ),
    )
    spread = (
        lax.broadcasted_iota(jnp.int32, (count, LANES), 1) % count
        == lax.broadcasted_iota(jnp.int32, (count, LANES), 0)
    ).astype(BF16)
    tags = jnp.dot(stack.astype(F32).astype(BF16), spread, preferred_element_type=F32)
    place = lax.broadcasted_iota(jnp.int32, (ROWS, LANES), 1) // count
    per_tile = LANES // count
    width = (edges[1] - edges[0]) * LANES
    tag_copies = []
    for step in range(size):
        mine = jnp.where(place == step % per_tile, tags, 0.0).astype(BF16)
        if step == 0:
            own_tag[...] = mine
            continue
        tagbuf[step] = mine
    for step in range(1, size):
        tag_copies.append(
            pltpu.make_async_copy(
                tagbuf.at[step],
                msgs[step - 1].at[:, pl.ds(groups * width, LANES)],
                tag_sems.at[step - 1],
            )
        )
        tag_copies[-1].start()
    for copy in copies + tag_copies:
        copy.wait()


def pack(images, classes, rotations, bins, cols, edges):
    size = lax.axis_size("mem")
    count = images.shape[0]
    groups = count // ROWS
    shapes = [jax.ShapeDtypeStruct((ROWS, LANES), BF16)]
    for chunk in range(len(edges) - 1):
        width = groups * (edges[chunk + 1] - edges[chunk]) * LANES + (LANES if chunk == 0 else 0)
        shapes += [jax.ShapeDtypeStruct((ROWS, width), BF16)] * (size - 1)
    total = (size - 1) * groups * (len(edges) - 1)
    outs = pl.pallas_call(
        functools.partial(pack_kernel, size, cols, edges),
        out_shape=shapes,
        in_specs=[ANY, VMEM, VMEM, VMEM],
        out_specs=[VMEM] + [ANY] * (len(shapes) - 1),
        scratch_shapes=[
            pltpu.VMEM((size, ROWS, LANES), BF16),
            pltpu.SemaphoreType.DMA((total,)),
            pltpu.SemaphoreType.DMA((size - 1,)),
        ],
        name="pack",
        **params(1 << 16, 4 * images.size),
    )(images, classes.reshape(1, -1), rotations.reshape(1, -1), bins.reshape(1, -1))
    own_tag, msgs = outs[0], outs[1:]
    return own_tag, [msgs[c * (size - 1) : (c + 1) * (size - 1)] for c in range(len(edges) - 1)]


def table_kernel(turns, ctf, pieces, weights, square):
    cols = ctf.shape[1]
    value = ctf[...]
    high = value.astype(BF16).astype(F32)
    mid = (value - high).astype(BF16).astype(F32)
    low = value - high - mid
    stacked = jnp.concatenate([high, mid, low], axis=0).astype(BF16)
    eye = identity()
    pick = (
        lax.broadcasted_iota(jnp.int32, (PIECES * BINS, PAIRS), 0) % BINS
        == lax.broadcasted_iota(jnp.int32, (PIECES * BINS, PAIRS), 1) % BINS
    ).astype(BF16)
    for tile in range(cols // LANES):
        rows = pl.ds(tile * LANES, LANES)
        flipped = lax.dot_general(
            eye, stacked[:, tile * LANES : (tile + 1) * LANES], NT, preferred_element_type=F32
        ).astype(BF16)
        pieces[rows, :] = flipped
        spread = jnp.dot(flipped, pick, preferred_element_type=F32)
        square[rows, :] = spread * spread
    per_tile = LANES // BINS
    turn = lax.broadcasted_iota(jnp.int32, (1, LANES), 1) // BINS
    levels = max(per_tile - 1, 1).bit_length()

    def one(q, carry):
        rows = pl.ds(pl.multiple_of(q * ANGLES, ROWS), ANGLES)
        for tile in range(PAIRS // LANES):
            block = turned(square[rows, pl.ds(tile * LANES, LANES)], SHIFT * per_tile * tile)
            for level in range(levels):
                chosen = (turn >> level & 1) == 1
                block = jnp.where(chosen, turned(block, SHIFT << level), block)
            high, low = split(block)
            weights[rows, pl.ds(tile * LANES, LANES)] = high
            weights[rows, pl.ds(PAIRS + tile * LANES, LANES)] = low
        return carry

    lax.fori_loop(0, turns, one, 0)


def tables(ctf, turns):
    cols = ctf.shape[1]
    return pl.pallas_call(
        functools.partial(table_kernel, turns),
        out_shape=[
            jax.ShapeDtypeStruct((cols, PIECES * BINS), BF16),
            jax.ShapeDtypeStruct((turns * ANGLES, 2 * PAIRS), BF16),
        ],
        in_specs=[VMEM],
        out_specs=[VMEM, VMEM],
        scratch_shapes=[pltpu.VMEM((cols, PAIRS), F32)],
        name="tables",
        **params(40 * cols * PAIRS, 4 * cols * PAIRS),
    )(ctf)


def numer_kernel(mem, cols, count, first, rows, base, tiles, segments, *refs):
    refs = list(refs)
    grp = lax.axis_size("grp")
    lanes = mem * count
    groups = count // ROWS
    img, pieces, tag_in = refs[:3]
    refs = refs[3:]
    msgs = []
    for _ in segments:
        msgs.append(refs[: mem - 1])
        refs = refs[mem - 1 :]
    if first:
        tags = refs.pop(0)
    else:
        tags = tag_in
    sums = refs[:grp]
    refs = refs[grp:]
    data, tagbuf, product, parts, sems, tag_sems = refs
    me = lax.axis_index("mem")
    own = lax.axis_index("grp")

    copies, tag_copies = [], []
    start = pl.multiple_of(me * cols + base * LANES, LANES)
    copies.append(
        pltpu.make_async_copy(
            img.at[:, pl.ds(start, tiles * LANES)], data.at[pl.ds(0, count)], sems.at[0]
        )
    )
    for seg, (wide, src, dst, width) in enumerate(segments):
        for step in range(1, mem):
            for g in range(groups):
                copies.append(
                    pltpu.make_async_copy(
                        msgs[seg][step - 1].at[:, pl.ds((g * wide + src) * LANES, width * LANES)],
                        data.at[
                            pl.ds(step * count + g * ROWS, ROWS), pl.ds(dst * LANES, width * LANES)
                        ],
                        sems.at[len(copies)],
                    )
                )
    if first:
        wide = segments[0][0]
        for step in range(1, mem):
            tag_copies.append(
                pltpu.make_async_copy(
                    msgs[0][step - 1].at[:, pl.ds(groups * wide * LANES, LANES)],
                    tagbuf.at[step],
                    tag_sems.at[step - 1],
                )
            )
    for copy in tag_copies + copies:
        copy.start()
    for copy in tag_copies:
        copy.wait()
    if first:
        per_tile = LANES // count
        for tile in range(lanes // LANES):
            total = None
            for step in range(tile * per_tile, (tile + 1) * per_tile):
                part = (tag_in[...] if step == 0 else tagbuf[step]).astype(F32)
                total = part if total is None else total + part
            tags[:, pl.ds(tile * LANES, LANES)] = total
    label = tags[...].astype(jnp.int32)
    key = label[0:1] * CPAD + label[1:2]
    spot = label[2:3]
    turn = label[3:4]
    pick = (
        lax.broadcasted_iota(jnp.int32, (PIECES * BINS, lanes), 0) % BINS == spot
    ).astype(BF16)
    klass = lax.broadcasted_iota(jnp.int32, (CPAD, lanes), 0)
    member = []
    for step in range(grp):
        one = (klass + CPAD * partner(own, step, grp) == key).astype(BF16)
        member.append(jnp.concatenate([one, one], axis=1))
    eye = identity()
    for copy in copies:
        copy.wait()

    def flip(tile, carry):
        across = pl.ds(pl.multiple_of(tile * LANES, LANES), LANES)
        flipped = lax.dot_general(eye, data[:, across], NT, preferred_element_type=F32)
        ctf = jnp.dot(
            pieces[pl.ds(pl.multiple_of((base + tile) * LANES, LANES), LANES), :],
            pick,
            preferred_element_type=F32,
        )
        product[across, :] = flipped * ctf
        return carry

    lax.fori_loop(0, tiles, flip, 0)
    offset = rows[0] * ANGLES - base * LANES

    def rotate(q, carry):
        for tile in range(lanes // LANES):
            block = product[
                pl.ds(pl.multiple_of(offset + q * ANGLES, ROWS), ANGLES),
                pl.ds(tile * LANES, LANES),
            ]
            bits = turn[:, tile * LANES : (tile + 1) * LANES]
            for level in range(LEVELS):
                chosen = (bits >> level & 1) == 1
                block = jnp.where(chosen, turned(block, SHIFT << level), block)
            high, low = split(block)
            where = pl.ds(pl.multiple_of(q * ANGLES, 2 * ROWS), ANGLES)
            parts[where, pl.ds(tile * LANES, LANES)] = high
            parts[where, pl.ds(lanes + tile * LANES, LANES)] = low
        return carry

    lax.fori_loop(0, rows[1] - rows[0], rotate, 0)
    result = lax.dot_general(
        jnp.concatenate(member, axis=0), parts[...], NT, preferred_element_type=F32
    )
    for step in range(grp):
        sums[step][...] = result[step * CPAD : (step + 1) * CPAD]


def numerators(images, pieces, tags, arrived, chunk, cols, edges, rows):
    mem, grp = lax.axis_size("mem"), lax.axis_size("grp")
    count = images.shape[0]
    first = chunk == 0
    here = (rows[chunk], rows[chunk + 1])
    base = here[0] * ANGLES // LANES
    stop = min(-(-here[1] * ANGLES // LANES), edges[-1])
    segments, msgs = [], []
    for c in range(chunk + 1):
        low, high = max(edges[c], base), min(edges[c + 1], stop)
        if low < high:
            segments.append((edges[c + 1] - edges[c], low - edges[c], low - base, high - low))
            msgs += arrived[c]
    lanes = mem * count
    span = (here[1] - here[0]) * ANGLES
    tiles = stop - base
    copies = 1 + len(segments) * (mem - 1) * (count // ROWS)
    shapes = [jax.ShapeDtypeStruct((ROWS, lanes), F32)] if first else []
    shapes += [jax.ShapeDtypeStruct((CPAD, span), F32)] * grp
    outs = pl.pallas_call(
        functools.partial(numer_kernel, mem, cols, count, first, here, base, tiles, tuple(segments)),
        out_shape=shapes,
        in_specs=[ANY, VMEM, VMEM] + [ANY] * len(msgs),
        out_specs=[VMEM] * len(shapes),
        scratch_shapes=[
            pltpu.VMEM((lanes, tiles * LANES), BF16),
            pltpu.VMEM((mem, ROWS, LANES), BF16),
            pltpu.VMEM((tiles * LANES, lanes), F32),
            pltpu.VMEM((span, 2 * lanes), BF16),
            pltpu.SemaphoreType.DMA((copies,)),
            pltpu.SemaphoreType.DMA((mem - 1,)),
        ],
        name="numerators",
        **params(40 * lanes * span + 4 * grp * CPAD * lanes * span, 8 * lanes * span),
    )(images, pieces, tags, *msgs)
    if first:
        return outs[0], outs[1:]
    return tags, outs


def denom_kernel(weights, *refs):
    tags, denom = refs[:-1], refs[-1]
    own = lax.axis_index("grp")
    lanes = tags[0].shape[1]
    klass = lax.broadcasted_iota(jnp.int32, (CPAD, lanes), 0)
    pair = lax.broadcasted_iota(jnp.int32, (PAIRS, lanes), 0)
    count = jnp.zeros((CPAD, PAIRS), F32)
    for ref in tags:
        label = ref[...].astype(jnp.int32)
        key = label[0:1] * CPAD + label[1:2]
        member = (klass + CPAD * own == key).astype(BF16)
        which = (pair == label[3:4] * BINS + label[2:3]).astype(BF16)
        count += lax.dot_general(member, which, NT, preferred_element_type=F32)
    high, low = split(count)
    left = jnp.concatenate(
        [jnp.concatenate([high, high], axis=1), jnp.concatenate([low, low], axis=1)], axis=0
    )
    both = lax.dot_general(left, weights[...], NT, preferred_element_type=F32)
    denom[...] = both[:CPAD] + both[CPAD:]


def denominators(weights, tags):
    span = weights.shape[0]
    lanes = tags[0].shape[1]
    return pl.pallas_call(
        denom_kernel,
        out_shape=jax.ShapeDtypeStruct((CPAD, span), F32),
        in_specs=[VMEM] * (1 + len(tags)),
        out_specs=VMEM,
        name="denominators",
        **params(4 * CPAD * span * PAIRS * 2 + len(tags) * lanes * PAIRS * 4, 4 * weights.size),
    )(weights, *tags)


def average_kernel(grp, rows, denom, *refs):
    sums, out = refs[:-1], refs[-1]
    for chunk in range(len(rows) - 1):
        across = pl.ds(rows[chunk] * ANGLES, (rows[chunk + 1] - rows[chunk]) * ANGLES)
        total = sums[chunk * grp][:CPG]
        for step in range(1, grp):
            total += sums[chunk * grp + step][:CPG]
        out[:, across] = total / (denom[:CPG, across] + wiener_term)


def averages(denom, sums, grp, rows):
    span = denom.shape[1]
    return pl.pallas_call(
        functools.partial(average_kernel, grp, rows),
        out_shape=jax.ShapeDtypeStruct((CPG, span), F32),
        in_specs=[VMEM] * (1 + len(sums)),
        out_specs=VMEM,
        name="averages",
        **params(8 * CPG * span, 4 * CPG * span * (grp + 2)),
    )(denom, *sums)


def plan(span):
    turns = span // ANGLES
    tiles = -(-span // LANES)
    edges = [0, tiles // 2, tiles] if tiles % 2 == 0 else [0, tiles]
    rows = [min(edge * LANES // ANGLES, turns) for edge in edges]
    return tuple(edges), tuple(rows)


def on_device(images, classes, rotations, bins, ctf_table):
    mem, grp = lax.axis_size("mem"), lax.axis_size("grp")
    count = images.shape[0]
    span = images.shape[1] // mem
    edges, rows = plan(span)
    cols = edges[-1] * LANES
    ctf = lax.dynamic_slice_in_dim(ctf_table, lax.axis_index("mem") * span, span, 1)
    if cols != span:
        images = jnp.pad(images.reshape(count, mem, span), ((0, 0), (0, 0), (0, cols - span)))
        images = images.reshape(count, mem * cols)
        ctf = jnp.pad(ctf, ((0, 0), (0, cols - span)))
    own_tag, packed = pack(images, classes, rotations, bins, cols, edges)
    arrived = [[send(msg, "mem", step + 1) for step, msg in enumerate(msgs)] for msgs in packed]
    pieces, weights = tables(ctf, span // ANGLES)
    tags, sums = own_tag, []
    for chunk in range(len(edges) - 1):
        tags, here = numerators(images, pieces, tags, arrived, chunk, cols, edges, rows)
        sums += [here[0]] + [send(here[step], "grp", step) for step in range(1, grp)]
    others = [send(tags, "grp", step) for step in range(1, grp)]
    denom = denominators(weights, [tags] + others)
    return averages(denom, sums, grp, rows)


def solution(mesh):
    in_specs = (
        P(("grp", "mem"), None),
        P(("grp", "mem")),
        P(("grp", "mem")),
        P(("grp", "mem")),
        P(),
    )
    out_specs = P("grp", "mem")
    return jax.shard_map(
        on_device, mesh=mesh, in_specs=in_specs, out_specs=out_specs, check_vma=False
    )
```

```python
import functools

import jax
import jax.numpy as jnp
from jax import lax
from jax.experimental import pallas as pl
from jax.experimental.pallas import tpu as pltpu
from jax.sharding import PartitionSpec as P

ANGLES = 144
ROTS = 36
BINS = 16
CPG = 50
SHIFT = 4

LANES = 128
ROWS = 8
CORES = 2
CPAD = -(-CPG // ROWS) * ROWS
PIECES = 3
NEAR = LANES // BINS
PAIRS = -(-ROTS // NEAR) * LANES
LEVELS = max(ROTS - 1, 1).bit_length()

wiener_term = 1.0

F32 = jnp.float32
BF16 = jnp.bfloat16
NT = (((1,), (1,)), ((), ()))
ANY = pl.BlockSpec(memory_space=pl.ANY)
HBM = pl.BlockSpec(memory_space=pltpu.HBM)
VMEM = pl.BlockSpec(memory_space=pltpu.VMEM)


def partner(index, step, size):
    if size & (size - 1) == 0:
        return index ^ step
    return lax.rem(index + step, size) if not isinstance(index, int) else (index + step) % size


def send(value, axis, step, cores=1):
    size = lax.axis_size(axis) // cores
    pairs = [
        (i * cores + core, partner(i, step, size) * cores + core)
        for i in range(size)
        for core in range(cores)
    ]
    return lax.ppermute(value, axis, pairs)


def swap(value, axis):
    return lax.ppermute(value, axis, [(i, i ^ 1) for i in range(lax.axis_size(axis))])


def identity():
    rows = lax.broadcasted_iota(jnp.int32, (LANES, LANES), 0)
    cols = lax.broadcasted_iota(jnp.int32, (LANES, LANES), 1)
    return (rows == cols).astype(BF16)


def turned(block, amount):
    amount %= ANGLES
    if amount == 0:
        return block
    if amount % ROWS == 0:
        return jnp.concatenate([block[amount:], block[:amount]], axis=0)
    return pltpu.roll(block, ANGLES - amount, 0)


def split(value):
    high = value.astype(BF16)
    low = (value - high.astype(F32)).astype(BF16)
    return high, low


def params(mebibytes):
    return dict(
        compiler_params=pltpu.CompilerParams(vmem_limit_bytes=mebibytes << 20),
        cost_estimate=pl.CostEstimate(flops=1 << 20, bytes_accessed=1 << 16, transcendentals=0),
    )


def run(copies, sems):
    copies = [
        pltpu.make_async_copy(src, dst, sems.at[spot]) for spot, (src, dst) in enumerate(copies)
    ]
    for copy in copies:
        copy.start()
    return copies


def pack_first_kernel(mem, cols, width, img, labels, *refs):
    places = mem // CORES
    outs, (data, sems) = refs[:places], refs[places:]
    count = data.shape[0]
    groups = count // ROWS
    here = lax.axis_index("mem") // CORES
    copies = run(
        [
            (img.at[:, pl.ds(dest * cols, width)], data.at[:, pl.ds(dest * width, width)])
            for dest in range(mem)
        ],
        sems,
    )
    label = labels[0:1]
    owner = jnp.zeros_like(label)
    for g in range(1, lax.axis_size("grp")):
        owner += (label >= g * CPG).astype(jnp.int32)
    row = lax.broadcasted_iota(jnp.int32, (ROWS, count), 0)
    stack = jnp.where(
        row == 0,
        owner,
        jnp.where(
            row == 1,
            label - owner * CPG,
            jnp.where(row == 2, labels[1:2], jnp.where(row == 3, labels[2:3], 0)),
        ),
    )
    spread = (
        lax.broadcasted_iota(jnp.int32, (count, LANES), 1) % count
        == lax.broadcasted_iota(jnp.int32, (count, LANES), 0)
    ).astype(BF16)
    tags = jnp.dot(stack.astype(F32).astype(BF16), spread, preferred_element_type=F32)
    place = lax.broadcasted_iota(jnp.int32, (ROWS, LANES), 1) // count
    for step in range(places):
        mine = jnp.where(place == step % (LANES // count), tags, 0.0)
        outs[step][:, pl.ds(CORES * groups * width, LANES)] = mine.astype(BF16)
    for copy in copies:
        copy.wait()
    for step in range(places):
        dest = partner(here, step, places) * CORES
        for core in range(CORES):
            start = pl.multiple_of((dest + core) * width, LANES)
            for g in range(groups):
                outs[step][:, pl.ds((core * groups + g) * width, width)] = data[
                    pl.ds(g * ROWS, ROWS), pl.ds(start, width)
                ]


def pack_first(images, classes, rotations, bins, cols, edges):
    mem = lax.axis_size("mem")
    count = images.shape[0]
    width = edges[1] * LANES
    shape = jax.ShapeDtypeStruct((ROWS, CORES * (count // ROWS) * width + LANES), BF16)
    return pl.pallas_call(
        functools.partial(pack_first_kernel, mem, cols, width),
        out_shape=[shape] * (mem // CORES),
        in_specs=[HBM, VMEM],
        out_specs=[VMEM] * (mem // CORES),
        scratch_shapes=[
            pltpu.VMEM((count, mem * width), BF16),
            pltpu.SemaphoreType.DMA((mem,)),
        ],
        name="pack_first",
        **params(8),
    )(images, jnp.stack([classes, bins, rotations]))


def cross_first_kernel(places, *refs):
    blocks, out = refs[:places], refs[-1]
    other = 1 - lax.rem(lax.axis_index("mem"), CORES)
    span = (blocks[0].shape[1] - LANES) // CORES
    for step, block in enumerate(blocks):
        out[step, :, pl.ds(0, span)] = block[:, pl.ds(pl.multiple_of(other * span, LANES), span)]
        out[step, :, pl.ds(span, LANES)] = block[:, pl.ds(CORES * span, LANES)]


def cross_first(blocks, after):
    span = (blocks[0].shape[1] - LANES) // CORES
    return pl.pallas_call(
        functools.partial(cross_first_kernel, len(blocks)),
        out_shape=jax.ShapeDtypeStruct((len(blocks), ROWS, span + LANES), BF16),
        in_specs=[VMEM] * len(blocks) + [ANY] * len(after),
        out_specs=VMEM,
        name="cross_first",
        **params(8),
    )(*blocks, *after)


def cross_later_kernel(mem, cols, low, width, img, out, data, sems):
    groups = data.shape[0] // ROWS
    places = mem // CORES
    here = lax.axis_index("mem") // CORES
    other = 1 - lax.rem(lax.axis_index("mem"), CORES)
    copies = []
    for step in range(places):
        dest = partner(here, step, places) * CORES + other
        start = pl.multiple_of(dest * cols + low, LANES)
        copies.append((img.at[:, pl.ds(start, width)], data.at[:, pl.ds(step * width, width)]))
    for step, copy in enumerate(run(copies, sems)):
        copy.wait()
        for g in range(groups):
            out[step, :, pl.ds(g * width, width)] = data[
                pl.ds(g * ROWS, ROWS), pl.ds(step * width, width)
            ]


def cross_later(images, cols, low, high):
    mem = lax.axis_size("mem")
    count = images.shape[0]
    width = (high - low) * LANES
    return pl.pallas_call(
        functools.partial(cross_later_kernel, mem, cols, low * LANES, width),
        out_shape=jax.ShapeDtypeStruct((mem // CORES, ROWS, count // ROWS * width), BF16),
        in_specs=[HBM],
        out_specs=VMEM,
        scratch_shapes=[
            pltpu.VMEM((count, mem // CORES * width), BF16),
            pltpu.SemaphoreType.DMA((mem // CORES,)),
        ],
        name="cross_later",
        **params(8),
    )(images)


def pack_later_kernel(mem, cols, low, width, img, crossed, after, *refs):
    places = mem // CORES
    outs, (data, sems) = refs[:places], refs[places:]
    groups = data.shape[0] // ROWS
    me = lax.axis_index("mem")
    here, core = me // CORES, lax.rem(me, CORES)
    copies = []
    for step in range(places):
        dest = partner(here, step, places) * CORES + core
        start = pl.multiple_of(dest * cols + low, LANES)
        copies.append((img.at[:, pl.ds(start, width)], data.at[:, pl.ds(step * width, width)]))
    copies = run(copies, sems)
    for step in range(places):
        outs[step][:, pl.ds(groups * width, groups * width)] = crossed[step]
    for step, copy in enumerate(copies):
        copy.wait()
        for g in range(groups):
            outs[step][:, pl.ds(g * width, width)] = data[
                pl.ds(g * ROWS, ROWS), pl.ds(step * width, width)
            ]


def pack_later(images, crossed, after, cols, low, high):
    mem = lax.axis_size("mem")
    places = mem // CORES
    count = images.shape[0]
    width = (high - low) * LANES
    shape = jax.ShapeDtypeStruct((ROWS, CORES * (count // ROWS) * width), BF16)
    return pl.pallas_call(
        functools.partial(pack_later_kernel, mem, cols, low * LANES, width),
        out_shape=[shape] * places,
        in_specs=[HBM, VMEM, ANY],
        out_specs=[VMEM] * places,
        scratch_shapes=[
            pltpu.VMEM((count, places * width), BF16),
            pltpu.SemaphoreType.DMA((places,)),
        ],
        name="pack_later",
        **params(8),
    )(images, crossed, after)


def table_kernel(turns, table, pieces, weights, ctf, square, sem):
    cols = ctf.shape[1]
    start = 0
    if table.shape[1] != cols:
        start = pl.multiple_of(lax.axis_index("mem") * cols, LANES)
    copy = pltpu.make_async_copy(table.at[:, pl.ds(start, cols)], ctf, sem)
    copy.start()
    copy.wait()
    value = ctf[...]
    high = value.astype(BF16).astype(F32)
    mid = (value - high).astype(BF16).astype(F32)
    low = value - high - mid
    stacked = jnp.concatenate([high, mid, low], axis=0).astype(BF16)
    eye = identity()
    pick = (
        lax.broadcasted_iota(jnp.int32, (PIECES * BINS, LANES), 0) % BINS
        == lax.broadcasted_iota(jnp.int32, (PIECES * BINS, LANES), 1) % BINS
    ).astype(BF16)
    for tile in range(cols // LANES):
        rows = pl.ds(tile * LANES, LANES)
        flipped = lax.dot_general(
            eye, stacked[:, tile * LANES : (tile + 1) * LANES], NT, preferred_element_type=F32
        ).astype(BF16)
        pieces[rows, :] = flipped
        spread = jnp.dot(flipped, pick, preferred_element_type=F32)
        square[rows, :] = spread * spread
    turn = lax.broadcasted_iota(jnp.int32, (1, LANES), 1) // BINS
    levels = max(NEAR - 1, 1).bit_length()

    def one(q, carry):
        rows = pl.ds(pl.multiple_of(q * ANGLES, 2 * ROWS), ANGLES)
        block = square[rows, :]
        for level in range(levels):
            chosen = (turn >> level & 1) == 1
            block = jnp.where(chosen, turned(block, SHIFT << level), block)
        high, low = split(block)
        weights[rows, pl.ds(0, LANES)] = high
        weights[rows, pl.ds(LANES, LANES)] = low
        return carry

    lax.fori_loop(0, turns, one, 0, unroll=2)


def tables(table, cols, turns):
    return pl.pallas_call(
        functools.partial(table_kernel, turns),
        out_shape=[
            jax.ShapeDtypeStruct((cols, PIECES * BINS), BF16),
            jax.ShapeDtypeStruct((turns * ANGLES, 2 * LANES), BF16),
        ],
        in_specs=[HBM],
        out_specs=[VMEM, VMEM],
        scratch_shapes=[
            pltpu.VMEM((BINS, cols), F32),
            pltpu.VMEM((cols, LANES), F32),
            pltpu.SemaphoreType.DMA,
        ],
        name="tables",
        **params(8),
    )(table)


def tag_spots(lanes, span):
    wide = span // LANES * LANES
    parts = -(-lanes // wide)
    spots = []
    for kind in range(3):
        for part in range(parts):
            spots.append((kind, CPG + kind * parts + part, part * wide, min(wide, lanes - part * wide)))
    return spots


def sum_rows(lanes, span):
    last = tag_spots(lanes, span)[-1][1] + 1
    return -(-last // ROWS) * ROWS


def read_tags(ref, lanes):
    kinds = [[], [], []]
    for kind, row, _, width in tag_spots(lanes, ref.shape[1]):
        kinds[kind].append(ref[pl.ds(row, 1), pl.ds(0, width)])
    return [jnp.concatenate(kind, axis=1) if len(kind) > 1 else kind[0] for kind in kinds]


def numer_kernel(mem, count, first, rows, base, tiles, segments, pieces, *refs):
    refs = list(refs)
    grp = lax.axis_size("grp")
    lanes = mem * count
    groups = count // ROWS
    places = mem // CORES
    core = lax.rem(lax.axis_index("mem"), CORES)
    own = lax.axis_index("grp")
    if not first:
        tags = refs.pop(0)
    for chunk, wide, src, dst, width in segments:
        across = pl.ds(dst * LANES, width * LANES)
        msgs, refs = refs[:places], refs[places:]
        if chunk == 0:
            crossed = refs.pop(0)
            past = groups * wide * LANES
        for step in range(places):
            for g in range(groups):
                low = (g * wide + src) * LANES
                if chunk == 0:
                    kept = pl.multiple_of(core * (groups * wide * LANES) + low, LANES)
                    near = msgs[step][:, pl.ds(kept, width * LANES)]
                    far = crossed[step, :, pl.ds(low, width * LANES)]
                else:
                    near = msgs[step][:, pl.ds(low, width * LANES)]
                    far = msgs[step][:, pl.ds(groups * wide * LANES + low, width * LANES)]
                refs[-3][pl.ds(step * count + g * ROWS, ROWS), across] = near
                refs[-3][pl.ds((places + step) * count + g * ROWS, ROWS), across] = far
    if first:
        tags = refs.pop(0)
        per_tile = LANES // count
        for tile in range(lanes // LANES):
            total = jnp.zeros((ROWS, LANES), F32)
            for slot in range(tile * per_tile, (tile + 1) * per_tile):
                if slot < places:
                    total += msgs[slot][:, pl.ds(CORES * past, LANES)].astype(F32)
                else:
                    total += crossed[slot - places, :, pl.ds(past, LANES)].astype(F32)
            tags[:, pl.ds(tile * LANES, LANES)] = total
    sums = refs[:grp]
    data, product, parts = refs[grp:]
    label = tags[...].astype(jnp.int32)
    key = label[0:1] * CPAD + label[1:2]
    spot = label[2:3]
    turn = label[3:4]
    pick = (
        lax.broadcasted_iota(jnp.int32, (PIECES * BINS, lanes), 0) % BINS == spot
    ).astype(BF16)
    klass = lax.broadcasted_iota(jnp.int32, (CPAD, lanes), 0)
    member = []
    for step in range(grp):
        one = (klass + CPAD * partner(own, step, grp) == key).astype(BF16)
        member.append(jnp.concatenate([one, one], axis=1))
    eye = identity()
    for tile in range(tiles):
        across = pl.ds(tile * LANES, LANES)
        flipped = lax.dot_general(eye, data[:, across], NT, preferred_element_type=F32)
        ctf = jnp.dot(
            pieces[pl.ds((base + tile) * LANES, LANES), :], pick, preferred_element_type=F32
        )
        product[across, :] = flipped * ctf
    offset = rows[0] * ANGLES - base * LANES

    def rotate(q, carry):
        for tile in range(lanes // LANES):
            block = product[
                pl.ds(pl.multiple_of(offset + q * ANGLES, ROWS), ANGLES),
                pl.ds(tile * LANES, LANES),
            ]
            bits = turn[:, tile * LANES : (tile + 1) * LANES]
            for level in range(LEVELS):
                chosen = (bits >> level & 1) == 1
                block = jnp.where(chosen, turned(block, SHIFT << level), block)
            high, low = split(block)
            where = pl.ds(pl.multiple_of(q * ANGLES, 2 * ROWS), ANGLES)
            parts[where, pl.ds(tile * LANES, LANES)] = high
            parts[where, pl.ds(lanes + tile * LANES, LANES)] = low
        return carry

    lax.fori_loop(0, rows[1] - rows[0], rotate, 0)
    result = lax.dot_general(
        jnp.concatenate(member, axis=0), parts[...], NT, preferred_element_type=F32
    )
    for step in range(grp):
        sums[step][pl.ds(0, CPAD)] = result[step * CPAD : (step + 1) * CPAD]
        if first:
            target = partner(own, step, grp)
            local = jnp.where(label[0:1] == target, label[1:2], -1)
            kinds = [kind.astype(F32) for kind in (local, spot, turn)]
            for kind, row, low, width in tag_spots(lanes, sums[step].shape[1]):
                sums[step][pl.ds(row, 1), pl.ds(0, width)] = kinds[kind][:, low : low + width]


def numerators(count, pieces, tags, arrived, chunk, edges, rows):
    mem, grp = lax.axis_size("mem"), lax.axis_size("grp")
    first = chunk == 0
    here = (rows[chunk], rows[chunk + 1])
    base = here[0] * ANGLES // LANES
    stop = min(-(-here[1] * ANGLES // LANES), edges[-1])
    segments, msgs = [], []
    for c in range(chunk + 1):
        low, high = max(edges[c], base), min(edges[c + 1], stop)
        if low < high:
            segments.append((c, edges[c + 1] - edges[c], low - edges[c], low - base, high - low))
            msgs += arrived[c]
    lanes = mem * count
    span = (here[1] - here[0]) * ANGLES
    tiles = stop - base
    shapes = [jax.ShapeDtypeStruct((ROWS, lanes), F32)] if first else []
    tall = sum_rows(lanes, span) if first else CPAD
    shapes += [jax.ShapeDtypeStruct((tall, span), F32)] * grp
    operands = [pieces] + ([] if first else [tags]) + msgs
    outs = pl.pallas_call(
        functools.partial(numer_kernel, mem, count, first, here, base, tiles, tuple(segments)),
        out_shape=shapes,
        in_specs=[VMEM] * len(operands),
        out_specs=[VMEM] * len(shapes),
        scratch_shapes=[
            pltpu.VMEM((lanes, tiles * LANES), BF16),
            pltpu.VMEM((tiles * LANES, lanes), F32),
            pltpu.VMEM((span, 2 * lanes), BF16),
        ],
        name="numerators",
        **params(16),
    )(*operands)
    if first:
        return outs[0], outs[1:]
    return tags, outs


def denom_kernel(lanes, weights, *refs):
    sums, (denom, spread) = refs[:-2], refs[-2:]
    span = weights.shape[0]
    klass = lax.broadcasted_iota(jnp.int32, (CPAD, lanes), 0)
    pair = lax.broadcasted_iota(jnp.int32, (PAIRS, lanes), 0)
    count = jnp.zeros((CPAD, PAIRS), F32)
    for ref in sums:
        local, spot, turn = [label.astype(jnp.int32) for label in read_tags(ref, lanes)]
        member = (klass == local).astype(BF16)
        which = (pair == turn * BINS + spot).astype(BF16)
        count += lax.dot_general(member, which, NT, preferred_element_type=F32)
    high, low = split(count)
    left = jnp.concatenate(
        [jnp.concatenate([high, high], axis=1), jnp.concatenate([low, low], axis=1)], axis=0
    )

    def turn_far(q, carry):
        rows = pl.ds(pl.multiple_of(q * ANGLES, 2 * ROWS), ANGLES)
        block = weights[rows, :]
        for tile in range(PAIRS // LANES):
            far = turned(block, SHIFT * NEAR * tile)
            spread[rows, pl.ds(tile * LANES, LANES)] = far[:, :LANES]
            spread[rows, pl.ds(PAIRS + tile * LANES, LANES)] = far[:, LANES:]
        return carry

    lax.fori_loop(0, span // ANGLES, turn_far, 0)
    both = lax.dot_general(left, spread[...], NT, preferred_element_type=F32)
    denom[...] = both[:CPAD] + both[CPAD:]


def denominators(weights, sums, lanes):
    span = weights.shape[0]
    return pl.pallas_call(
        functools.partial(denom_kernel, lanes),
        out_shape=jax.ShapeDtypeStruct((CPAD, span), F32),
        in_specs=[VMEM] * (1 + len(sums)),
        out_specs=VMEM,
        scratch_shapes=[pltpu.VMEM((span, 2 * PAIRS), BF16)],
        name="denominators",
        **params(20),
    )(weights, *sums)


def average_kernel(grp, rows, denom, *refs):
    sums, out = refs[:-1], refs[-1]
    for chunk in range(len(rows) - 1):
        across = pl.ds(rows[chunk] * ANGLES, (rows[chunk + 1] - rows[chunk]) * ANGLES)
        total = sums[chunk * grp][:CPG]
        for step in range(1, grp):
            total += sums[chunk * grp + step][:CPG]
        out[:, across] = total / (denom[:CPG, across] + wiener_term)


def averages(denom, sums, grp, rows):
    span = denom.shape[1]
    return pl.pallas_call(
        functools.partial(average_kernel, grp, rows),
        out_shape=jax.ShapeDtypeStruct((CPG, span), F32),
        in_specs=[VMEM] * (1 + len(sums)),
        out_specs=VMEM,
        name="averages",
        **params(8),
    )(denom, *sums)


def plan(span):
    turns = span // ANGLES
    tiles = -(-span // LANES)
    edges = [0, tiles // 2, tiles] if tiles % 2 == 0 else [0, tiles]
    rows = [min(edge * LANES // ANGLES, turns) for edge in edges]
    return tuple(edges), tuple(rows)


def on_device(images, classes, rotations, bins, ctf_table):
    mem, grp = lax.axis_size("mem"), lax.axis_size("grp")
    count = images.shape[0]
    span = images.shape[1] // mem
    edges, rows = plan(span)
    cols = edges[-1] * LANES
    places = mem // CORES
    table = ctf_table
    if cols != span:
        images = jnp.pad(images.reshape(count, mem, span), ((0, 0), (0, 0), (0, cols - span)))
        images = images.reshape(count, mem * cols)
        table = lax.dynamic_slice_in_dim(ctf_table, lax.axis_index("mem") * span, span, 1)
        table = jnp.pad(table, ((0, 0), (0, cols - span)))
    pieces, weights = tables(table, cols, span // ANGLES)
    steps = pack_first(images, classes, rotations, bins, cols, edges)
    here = {step: send(steps[step], "mem", step, CORES) for step in range(places - 1, 0, -1)}
    here[0] = steps[0]
    first = [here[step] for step in range(places)]
    after, arrived, ties = first[-1], [], [pieces]
    for low, high in zip(edges[1:], edges[2:]):
        crossed = swap(cross_later(images, cols, low, high), "mem")
        steps = pack_later(images, crossed, after, cols, low, high)
        here = {step: send(steps[step], "mem", step, CORES) for step in range(places - 1, 0, -1)}
        here[0] = steps[0]
        after = here[places - 1]
        ties.append(steps[0])
        arrived.append([here[step] for step in range(places)])
    arrived = [first + [swap(cross_first(first, ties[:2]), "mem")]] + arrived
    tags, sums = None, []
    for chunk in range(len(edges) - 1):
        tags, here = numerators(count, pieces, tags, arrived, chunk, edges, rows)
        sums += [here[0]] + [send(here[step], "grp", step) for step in range(1, grp)]
    denom = denominators(weights, sums[:grp], mem * count)
    return averages(denom, sums, grp, rows)


def solution(mesh):
    in_specs = (
        P(("grp", "mem"), None),
        P(("grp", "mem")),
        P(("grp", "mem")),
        P(("grp", "mem")),
        P(),
    )
    out_specs = P("grp", "mem")
    return jax.shard_map(
        on_device, mesh=mesh, in_specs=in_specs, out_specs=out_specs, check_vma=False
    )
```

```python
import functools

import jax
import jax.numpy as jnp
from jax import lax
from jax.experimental import pallas as pl
from jax.experimental.pallas import tpu as pltpu
from jax.sharding import PartitionSpec as P

ANGLES = 144
ROTS = 36
BINS = 16
CPG = 50
SHIFT = 4

LANES = 128
ROWS = 8
CORES = 2
CPAD = -(-CPG // ROWS) * ROWS
PIECES = 3
NEAR = LANES // BINS
PAIRS = -(-ROTS // NEAR) * LANES
LEVELS = max(ROTS - 1, 1).bit_length()

wiener_term = 1.0

F32 = jnp.float32
BF16 = jnp.bfloat16
HALF = jnp.float16
NT = (((1,), (1,)), ((), ()))
ANY = pl.BlockSpec(memory_space=pl.ANY)
HBM = pl.BlockSpec(memory_space=pltpu.HBM)
VMEM = pl.BlockSpec(memory_space=pltpu.VMEM)


def partner(index, step, size):
    if size & (size - 1) == 0:
        return index ^ step
    return lax.rem(index + step, size) if not isinstance(index, int) else (index + step) % size


def send(value, axis, step, cores=1, cross=0):
    size = lax.axis_size(axis) // cores
    pairs = [
        (i * cores + core, partner(i, step, size) * cores + (core ^ cross))
        for i in range(size)
        for core in range(cores)
    ]
    return lax.ppermute(value, axis, pairs)


def identity():
    rows = lax.broadcasted_iota(jnp.int32, (LANES, LANES), 0)
    cols = lax.broadcasted_iota(jnp.int32, (LANES, LANES), 1)
    return (rows == cols).astype(BF16)


def turned(block, amount):
    amount %= ANGLES
    if amount == 0:
        return block
    if amount % ROWS == 0:
        return jnp.concatenate([block[amount:], block[:amount]], axis=0)
    return pltpu.roll(block, ANGLES - amount, 0)


def split(value):
    high = value.astype(BF16)
    low = (value - high.astype(F32)).astype(BF16)
    return high, low


def params(mebibytes):
    return dict(
        compiler_params=pltpu.CompilerParams(vmem_limit_bytes=mebibytes << 20),
        cost_estimate=pl.CostEstimate(flops=1 << 20, bytes_accessed=1 << 16, transcendentals=0),
    )


def pack_kernel(mem, cols, edges, img, labels, *outs):
    places = mem // CORES
    count = img.shape[0]
    groups = count // ROWS
    here = lax.axis_index("mem") // CORES
    core = lax.rem(lax.axis_index("mem"), CORES)
    label = labels[0:1]
    owner = jnp.zeros_like(label)
    for g in range(1, lax.axis_size("grp")):
        owner += (label >= g * CPG).astype(jnp.int32)
    row = lax.broadcasted_iota(jnp.int32, (ROWS, count), 0)
    stack = jnp.where(
        row == 0,
        owner,
        jnp.where(
            row == 1,
            label - owner * CPG,
            jnp.where(row == 2, labels[1:2], jnp.where(row == 3, labels[2:3], 0)),
        ),
    )
    spread = (
        lax.broadcasted_iota(jnp.int32, (count, LANES), 1) % count
        == lax.broadcasted_iota(jnp.int32, (count, LANES), 0)
    ).astype(BF16)
    tags = jnp.dot(stack.astype(F32).astype(BF16), spread, preferred_element_type=F32)
    place = lax.broadcasted_iota(jnp.int32, (ROWS, LANES), 1) // count
    first = (edges[1] - edges[0]) * LANES
    for step in range(places):
        there = partner(here, step, places) * CORES
        for target in range(CORES):
            start = pl.multiple_of((there + target) * cols + edges[0] * LANES, LANES)
            for g in range(groups):
                outs[step][:, pl.ds((target * groups + g) * first, first)] = img[
                    pl.ds(g * ROWS, ROWS), pl.ds(start, first)
                ]
        mine = jnp.where(place == step % (LANES // count), tags, 0.0)
        outs[step][:, pl.ds(CORES * groups * first, LANES)] = mine.astype(BF16)
        if len(edges) == 2:
            continue
        width = (edges[2] - edges[1]) * LANES
        for cross in range(CORES):
            start = pl.multiple_of((there + (core ^ cross)) * cols + edges[1] * LANES, LANES)
            for g in range(groups):
                outs[places + cross][step, :, pl.ds(g * width, width)] = img[
                    pl.ds(g * ROWS, ROWS), pl.ds(start, width)
                ]


def pack(images, labels, cols, edges):
    mem = lax.axis_size("mem")
    groups = images.shape[0] // ROWS
    wide = [groups * (high - low) * LANES for low, high in zip(edges, edges[1:])]
    shapes = [jax.ShapeDtypeStruct((ROWS, CORES * wide[0] + LANES), BF16)] * (mem // CORES)
    for width in wide[1:]:
        shapes += [jax.ShapeDtypeStruct((mem // CORES, ROWS, width), BF16)] * CORES
    outs = pl.pallas_call(
        functools.partial(pack_kernel, mem, cols, edges),
        out_shape=shapes,
        in_specs=[VMEM] * 2,
        out_specs=[VMEM] * len(shapes),
        name="pack",
        **params(8),
    )(images, labels)
    return outs[: mem // CORES], outs[mem // CORES :]


def join_kernel(kept, crossed, *refs):
    places, _, span = kept.shape
    outs = refs[-places:]
    for step in range(places):
        outs[step][:, pl.ds(0, span)] = kept[step]
        outs[step][:, pl.ds(span, span)] = crossed[step]


def join(kept, crossed, after):
    places, _, span = kept.shape
    return pl.pallas_call(
        join_kernel,
        out_shape=[jax.ShapeDtypeStruct((ROWS, CORES * span), BF16)] * places,
        in_specs=[VMEM] * 2 + [ANY] * len(after),
        out_specs=[VMEM] * places,
        name="join",
        **params(8),
    )(kept, crossed, *after)


def cross_kernel(places, *refs):
    blocks, out = refs[:places], refs[-1]
    other = 1 - lax.rem(lax.axis_index("mem"), CORES)
    span = (blocks[0].shape[1] - LANES) // CORES
    for step, block in enumerate(blocks):
        out[step, :, pl.ds(0, span)] = block[:, pl.ds(pl.multiple_of(other * span, LANES), span)]
        out[step, :, pl.ds(span, LANES)] = block[:, pl.ds(CORES * span, LANES)]


def cross(blocks, after):
    span = (blocks[0].shape[1] - LANES) // CORES
    return pl.pallas_call(
        functools.partial(cross_kernel, len(blocks)),
        out_shape=jax.ShapeDtypeStruct((len(blocks), ROWS, span + LANES), BF16),
        in_specs=[VMEM] * len(blocks) + [ANY] * len(after),
        out_specs=VMEM,
        name="cross",
        **params(8),
    )(*blocks, *after)


def table_kernel(turns, table, pieces, weights, ctf, square, sem):
    cols = ctf.shape[1]
    start = 0
    if table.shape[1] != cols:
        start = pl.multiple_of(lax.axis_index("mem") * cols, LANES)
    copy = pltpu.make_async_copy(table.at[:, pl.ds(start, cols)], ctf, sem)
    copy.start()
    copy.wait()
    value = ctf[...]
    high = value.astype(BF16).astype(F32)
    mid = (value - high).astype(BF16).astype(F32)
    low = value - high - mid
    stacked = jnp.concatenate([high, mid, low], axis=0).astype(BF16)
    eye = identity()
    pick = (
        lax.broadcasted_iota(jnp.int32, (PIECES * BINS, LANES), 0) % BINS
        == lax.broadcasted_iota(jnp.int32, (PIECES * BINS, LANES), 1) % BINS
    ).astype(BF16)
    for tile in range(cols // LANES):
        rows = pl.ds(tile * LANES, LANES)
        flipped = lax.dot_general(
            eye, stacked[:, tile * LANES : (tile + 1) * LANES], NT, preferred_element_type=F32
        ).astype(BF16)
        pieces[rows, :] = flipped
        spread = jnp.dot(flipped, pick, preferred_element_type=F32)
        square[rows, :] = spread * spread
    turn = lax.broadcasted_iota(jnp.int32, (1, LANES), 1) // BINS
    levels = max(NEAR - 1, 1).bit_length()

    def one(q, carry):
        rows = pl.ds(pl.multiple_of(q * ANGLES, 2 * ROWS), ANGLES)
        block = square[rows, :]
        for level in range(levels):
            chosen = (turn >> level & 1) == 1
            block = jnp.where(chosen, turned(block, SHIFT << level), block)
        high, low = split(block)
        weights[rows, pl.ds(0, LANES)] = high
        weights[rows, pl.ds(LANES, LANES)] = low
        return carry

    lax.fori_loop(0, turns, one, 0, unroll=2)


def tables(table, cols, turns):
    return pl.pallas_call(
        functools.partial(table_kernel, turns),
        out_shape=[
            jax.ShapeDtypeStruct((cols, PIECES * BINS), BF16),
            jax.ShapeDtypeStruct((turns * ANGLES, 2 * LANES), BF16),
        ],
        in_specs=[HBM],
        out_specs=[VMEM, VMEM],
        scratch_shapes=[
            pltpu.VMEM((BINS, cols), F32),
            pltpu.VMEM((cols, LANES), F32),
            pltpu.SemaphoreType.DMA,
        ],
        name="tables",
        **params(8),
    )(table)


def tag_spots(lanes, span):
    wide = span // LANES * LANES
    parts = -(-lanes // wide)
    spots = []
    for kind in range(3):
        for part in range(parts):
            spots.append((kind, CPG + kind * parts + part, part * wide, min(wide, lanes - part * wide)))
    return spots


def sum_rows(lanes, span):
    last = tag_spots(lanes, span)[-1][1] + 1
    return -(-last // ROWS) * ROWS


def tag_block(message, lanes):
    low = CPG // ROWS * ROWS
    return message[low:].astype(F32)


def read_tags(ref, lanes):
    kinds = [[], [], []]
    for kind, row, _, width in tag_spots(lanes, ref.shape[1]):
        kinds[kind].append(ref[pl.ds(row - CPG // ROWS * ROWS, 1), pl.ds(0, width)])
    return [jnp.concatenate(kind, axis=1) if len(kind) > 1 else kind[0] for kind in kinds]


def numer_kernel(mem, count, first, rows, base, tiles, segments, pieces, *refs):
    refs = list(refs)
    grp = lax.axis_size("grp")
    lanes = mem * count
    groups = count // ROWS
    places = mem // CORES
    core = lax.rem(lax.axis_index("mem"), CORES)
    own = lax.axis_index("grp")
    if not first:
        tags = refs.pop(0)
    for chunk, wide, src, dst, width in segments:
        across = pl.ds(dst * LANES, width * LANES)
        msgs, refs = refs[:places], refs[places:]
        if chunk == 0:
            crossed = refs.pop(0)
            past = groups * wide * LANES
        for step in range(places):
            for g in range(groups):
                low = (g * wide + src) * LANES
                if chunk == 0:
                    kept = pl.multiple_of(core * (groups * wide * LANES) + low, LANES)
                    near = msgs[step][:, pl.ds(kept, width * LANES)]
                    far = crossed[step, :, pl.ds(low, width * LANES)]
                else:
                    near = msgs[step][:, pl.ds(low, width * LANES)]
                    far = msgs[step][:, pl.ds(groups * wide * LANES + low, width * LANES)]
                refs[-3][pl.ds(step * count + g * ROWS, ROWS), across] = near
                refs[-3][pl.ds((places + step) * count + g * ROWS, ROWS), across] = far
    if first:
        tags = refs.pop(0)
        per_tile = LANES // count
        for tile in range(lanes // LANES):
            total = jnp.zeros((ROWS, LANES), F32)
            for slot in range(tile * per_tile, (tile + 1) * per_tile):
                if slot < places:
                    total += msgs[slot][:, pl.ds(CORES * past, LANES)].astype(F32)
                else:
                    total += crossed[slot - places, :, pl.ds(past, LANES)].astype(F32)
            tags[:, pl.ds(tile * LANES, LANES)] = total
    sums = refs[:grp]
    data, product, parts = refs[grp:]
    label = tags[...].astype(jnp.int32)
    key = label[0:1] * CPAD + label[1:2]
    spot = label[2:3]
    turn = label[3:4]
    pick = (
        lax.broadcasted_iota(jnp.int32, (PIECES * BINS, lanes), 0) % BINS == spot
    ).astype(BF16)
    klass = lax.broadcasted_iota(jnp.int32, (CPAD, lanes), 0)
    member = []
    for step in range(grp):
        one = (klass + CPAD * partner(own, step, grp) == key).astype(BF16)
        member.append(jnp.concatenate([one, one], axis=1))
    eye = identity()
    for tile in range(tiles):
        across = pl.ds(tile * LANES, LANES)
        flipped = lax.dot_general(eye, data[:, across], NT, preferred_element_type=F32)
        ctf = jnp.dot(
            pieces[pl.ds((base + tile) * LANES, LANES), :], pick, preferred_element_type=F32
        )
        product[across, :] = flipped * ctf
    offset = rows[0] * ANGLES - base * LANES

    def rotate(q, carry):
        for tile in range(lanes // LANES):
            block = product[
                pl.ds(pl.multiple_of(offset + q * ANGLES, ROWS), ANGLES),
                pl.ds(tile * LANES, LANES),
            ]
            bits = turn[:, tile * LANES : (tile + 1) * LANES]
            for level in range(LEVELS):
                chosen = (bits >> level & 1) == 1
                block = jnp.where(chosen, turned(block, SHIFT << level), block)
            high, low = split(block)
            where = pl.ds(pl.multiple_of(q * ANGLES, 2 * ROWS), ANGLES)
            parts[where, pl.ds(tile * LANES, LANES)] = high
            parts[where, pl.ds(lanes + tile * LANES, LANES)] = low
        return carry

    lax.fori_loop(0, rows[1] - rows[0], rotate, 0)
    result = lax.dot_general(
        jnp.concatenate(member, axis=0), parts[...], NT, preferred_element_type=F32
    )
    for step in range(grp):
        sums[step][pl.ds(0, CPAD)] = result[step * CPAD : (step + 1) * CPAD]
        if first:
            target = partner(own, step, grp)
            local = jnp.where(label[0:1] == target, label[1:2], -1)
            kinds = [kind.astype(F32) for kind in (local, spot, turn)]
            for kind, row, low, width in tag_spots(lanes, sums[step].shape[1]):
                sums[step][pl.ds(row, 1), pl.ds(0, width)] = kinds[kind][:, low : low + width]


def numerators(count, pieces, tags, arrived, chunk, edges, rows):
    mem, grp = lax.axis_size("mem"), lax.axis_size("grp")
    first = chunk == 0
    here = (rows[chunk], rows[chunk + 1])
    base = here[0] * ANGLES // LANES
    stop = min(-(-here[1] * ANGLES // LANES), edges[-1])
    segments, msgs = [], []
    for c in range(chunk + 1):
        low, high = max(edges[c], base), min(edges[c + 1], stop)
        if low < high:
            segments.append((c, edges[c + 1] - edges[c], low - edges[c], low - base, high - low))
            msgs += arrived[c]
    lanes = mem * count
    span = (here[1] - here[0]) * ANGLES
    tiles = stop - base
    shapes = [jax.ShapeDtypeStruct((ROWS, lanes), F32)] if first else []
    tall = sum_rows(lanes, span) if first else CPAD
    shapes += [jax.ShapeDtypeStruct((tall, span), F32)] * grp
    operands = [pieces] + ([] if first else [tags]) + msgs
    outs = pl.pallas_call(
        functools.partial(numer_kernel, mem, count, first, here, base, tiles, tuple(segments)),
        out_shape=shapes,
        in_specs=[VMEM] * len(operands),
        out_specs=[VMEM] * len(shapes),
        scratch_shapes=[
            pltpu.VMEM((lanes, tiles * LANES), BF16),
            pltpu.VMEM((tiles * LANES, lanes), F32),
            pltpu.VMEM((span, 2 * lanes), BF16),
        ],
        name="numerators",
        **params(16),
    )(*operands)
    if first:
        return outs[0], outs[1:]
    return tags, outs


def denom_kernel(lanes, weights, *refs):
    blocks, (denom, spread) = refs[:-2], refs[-2:]
    span = weights.shape[0]
    klass = lax.broadcasted_iota(jnp.int32, (CPAD, lanes), 0)
    pair = lax.broadcasted_iota(jnp.int32, (PAIRS, lanes), 0)
    count = jnp.zeros((CPAD, PAIRS), F32)
    for ref in blocks:
        local, spot, turn = [label.astype(jnp.int32) for label in read_tags(ref, lanes)]
        member = (klass == local).astype(BF16)
        which = (pair == turn * BINS + spot).astype(BF16)
        count += lax.dot_general(member, which, NT, preferred_element_type=F32)
    high, low = split(count)
    left = jnp.concatenate(
        [jnp.concatenate([high, high], axis=1), jnp.concatenate([low, low], axis=1)], axis=0
    )

    def turn_far(q, carry):
        rows = pl.ds(pl.multiple_of(q * ANGLES, 2 * ROWS), ANGLES)
        block = weights[rows, :]
        for tile in range(PAIRS // LANES):
            far = turned(block, SHIFT * NEAR * tile)
            spread[rows, pl.ds(tile * LANES, LANES)] = far[:, :LANES]
            spread[rows, pl.ds(PAIRS + tile * LANES, LANES)] = far[:, LANES:]
        return carry

    lax.fori_loop(0, span // ANGLES, turn_far, 0)
    both = lax.dot_general(left, spread[...], NT, preferred_element_type=F32)
    denom[...] = both[:CPAD] + both[CPAD:]


def denominators(weights, blocks, lanes):
    span = weights.shape[0]
    return pl.pallas_call(
        functools.partial(denom_kernel, lanes),
        out_shape=jax.ShapeDtypeStruct((CPAD, span), F32),
        in_specs=[VMEM] * (1 + len(blocks)),
        out_specs=VMEM,
        scratch_shapes=[pltpu.VMEM((span, 2 * PAIRS), BF16)],
        name="denominators",
        **params(20),
    )(weights, *blocks)


def average_kernel(rows, denom, *refs):
    sums, out = refs[:-1], refs[-1]
    for chunk in range(len(rows) - 1):
        across = pl.ds(rows[chunk] * ANGLES, (rows[chunk + 1] - rows[chunk]) * ANGLES)
        out[:, across] = sums[chunk][:CPG] / (denom[:CPG, across] + wiener_term)


def averages(denom, sums, rows):
    span = denom.shape[1]
    return pl.pallas_call(
        functools.partial(average_kernel, rows),
        out_shape=jax.ShapeDtypeStruct((CPG, span), F32),
        in_specs=[VMEM] * (1 + len(sums)),
        out_specs=VMEM,
        name="averages",
        **params(8),
    )(denom, *sums)


def plan(span):
    turns = span // ANGLES
    tiles = -(-span // LANES)
    edges = [0, tiles // 2, tiles] if tiles % 2 == 0 else [0, tiles]
    rows = [min(edge * LANES // ANGLES, turns) for edge in edges]
    return tuple(edges), tuple(rows)


def on_device(images, classes, rotations, bins, ctf_table):
    mem, grp = lax.axis_size("mem"), lax.axis_size("grp")
    count = images.shape[0]
    span = images.shape[1] // mem
    edges, rows = plan(span)
    cols = edges[-1] * LANES
    places = mem // CORES
    table = ctf_table
    if cols != span:
        images = jnp.pad(images.reshape(count, mem, span), ((0, 0), (0, 0), (0, cols - span)))
        images = images.reshape(count, mem * cols)
        table = lax.dynamic_slice_in_dim(ctf_table, lax.axis_index("mem") * span, span, 1)
        table = jnp.pad(table, ((0, 0), (0, cols - span)))
    pieces, weights = tables(table, cols, span // ANGLES)
    firsts, seconds = pack(images, jnp.stack([classes, bins, rotations]), cols, edges)
    others = range(places - 1, 0, -1)
    here = {step: send(firsts[step], "mem", step, CORES) for step in others}
    here[0] = firsts[0]
    first = [here[step] for step in range(places)]
    arrived, after = [], [pieces]
    if seconds:
        kept, crossed = seconds[0], send(seconds[1], "mem", 0, CORES, 1)
        msgs = join(kept, crossed, [first[-1], pieces])
        here = {step: send(msgs[step], "mem", step, CORES) for step in others}
        here[0] = msgs[0]
        arrived, after = [[here[step] for step in range(places)]], [msgs[0]]
    arrived = [first + [send(cross(first, after), "mem", 0, CORES, 1)]] + arrived
    tags, sums, blocks = None, [], []
    for chunk in range(len(edges) - 1):
        tags, here = numerators(count, pieces, tags, arrived, chunk, edges, rows)
        others = [send(here[step].astype(HALF), "grp", step) for step in range(1, grp)]
        if chunk == 0:
            blocks = [tag_block(part, mem * count) for part in [here[0]] + others]
        total = here[0]
        for part in others:
            total = total + part.astype(F32)
        sums.append(total)
    denom = denominators(weights, blocks, mem * count)
    return averages(denom, sums, rows)


def solution(mesh):
    in_specs = (
        P(("grp", "mem"), None),
        P(("grp", "mem")),
        P(("grp", "mem")),
        P(("grp", "mem")),
        P(),
    )
    out_specs = P("grp", "mem")
    return jax.shard_map(
        on_device, mesh=mesh, in_specs=in_specs, out_specs=out_specs, check_vma=False
    )
```

```python
import functools

import jax
import jax.numpy as jnp
from jax import lax
from jax.experimental import pallas as pl
from jax.experimental.pallas import tpu as pltpu
from jax.sharding import PartitionSpec as P

ANGLES = 144
ROTS = 36
BINS = 16
CPG = 50
SHIFT = 4

LANES = 128
ROWS = 8
CORES = 2
CPAD = -(-CPG // ROWS) * ROWS
PIECES = 3
NEAR = LANES // BINS
PAIRS = -(-ROTS // NEAR) * LANES
LEVELS = max(ROTS - 1, 1).bit_length()

wiener_term = 1.0

F32 = jnp.float32
BF16 = jnp.bfloat16
HALF = jnp.float16
NT = (((1,), (1,)), ((), ()))
ANY = pl.BlockSpec(memory_space=pl.ANY)
HBM = pl.BlockSpec(memory_space=pltpu.HBM)
VMEM = pl.BlockSpec(memory_space=pltpu.VMEM)


def partner(index, step, size):
    if size & (size - 1) == 0:
        return index ^ step
    return lax.rem(index + step, size) if not isinstance(index, int) else (index + step) % size


def send(value, axis, step, cores=1, cross=0):
    size = lax.axis_size(axis) // cores
    pairs = [
        (i * cores + core, partner(i, step, size) * cores + (core ^ cross))
        for i in range(size)
        for core in range(cores)
    ]
    return lax.ppermute(value, axis, pairs)


def identity():
    rows = lax.broadcasted_iota(jnp.int32, (LANES, LANES), 0)
    cols = lax.broadcasted_iota(jnp.int32, (LANES, LANES), 1)
    return (rows == cols).astype(BF16)


def turned(block, amount):
    amount %= ANGLES
    if amount == 0:
        return block
    if amount % ROWS == 0:
        return jnp.concatenate([block[amount:], block[:amount]], axis=0)
    return pltpu.roll(block, ANGLES - amount, 0)


def split(value):
    high = value.astype(BF16)
    low = (value - high.astype(F32)).astype(BF16)
    return high, low


def params(mebibytes):
    return dict(
        compiler_params=pltpu.CompilerParams(vmem_limit_bytes=mebibytes << 20),
        cost_estimate=pl.CostEstimate(flops=1 << 20, bytes_accessed=1 << 16, transcendentals=0),
    )


def pack_kernel(mem, cols, edges, img, labels, *outs):
    places = mem // CORES
    count = img.shape[0]
    groups = count // ROWS
    here = lax.axis_index("mem") // CORES
    core = lax.rem(lax.axis_index("mem"), CORES)
    label = labels[0:1]
    owner = jnp.zeros_like(label)
    for g in range(1, lax.axis_size("grp")):
        owner += (label >= g * CPG).astype(jnp.int32)
    row = lax.broadcasted_iota(jnp.int32, (ROWS, count), 0)
    stack = jnp.where(
        row == 0,
        owner,
        jnp.where(
            row == 1,
            label - owner * CPG,
            jnp.where(row == 2, labels[1:2], jnp.where(row == 3, labels[2:3], 0)),
        ),
    )
    spread = (
        lax.broadcasted_iota(jnp.int32, (count, LANES), 1) % count
        == lax.broadcasted_iota(jnp.int32, (count, LANES), 0)
    ).astype(BF16)
    tags = jnp.dot(stack.astype(F32).astype(BF16), spread, preferred_element_type=F32)
    place = lax.broadcasted_iota(jnp.int32, (ROWS, LANES), 1) // count
    first = (edges[1] - edges[0]) * LANES
    for step in range(places):
        there = partner(here, step, places) * CORES
        for target in range(CORES):
            start = pl.multiple_of((there + target) * cols + edges[0] * LANES, LANES)
            for g in range(groups):
                outs[step][:, pl.ds((target * groups + g) * first, first)] = img[
                    pl.ds(g * ROWS, ROWS), pl.ds(start, first)
                ]
        mine = jnp.where(place == step % (LANES // count), tags, 0.0)
        outs[step][:, pl.ds(CORES * groups * first, LANES)] = mine.astype(BF16)
        if len(edges) == 2:
            continue
        width = (edges[2] - edges[1]) * LANES
        for cross in range(CORES):
            start = pl.multiple_of((there + (core ^ cross)) * cols + edges[1] * LANES, LANES)
            for g in range(groups):
                outs[places + cross][step, :, pl.ds(g * width, width)] = img[
                    pl.ds(g * ROWS, ROWS), pl.ds(start, width)
                ]


def pack(images, labels, cols, edges):
    mem = lax.axis_size("mem")
    groups = images.shape[0] // ROWS
    wide = [groups * (high - low) * LANES for low, high in zip(edges, edges[1:])]
    shapes = [jax.ShapeDtypeStruct((ROWS, CORES * wide[0] + LANES), BF16)] * (mem // CORES)
    for width in wide[1:]:
        shapes += [jax.ShapeDtypeStruct((mem // CORES, ROWS, width), BF16)] * CORES
    outs = pl.pallas_call(
        functools.partial(pack_kernel, mem, cols, edges),
        out_shape=shapes,
        in_specs=[VMEM] * 2,
        out_specs=[VMEM] * len(shapes),
        name="pack",
        **params(8),
    )(images, labels)
    return outs[: mem // CORES], outs[mem // CORES :]


def join_kernel(kept, crossed, *refs):
    places, _, span = kept.shape
    outs = refs[-places:]
    for step in range(places):
        outs[step][:, pl.ds(0, span)] = kept[step]
        outs[step][:, pl.ds(span, span)] = crossed[step]


def join(kept, crossed, after):
    places, _, span = kept.shape
    return pl.pallas_call(
        join_kernel,
        out_shape=[jax.ShapeDtypeStruct((ROWS, CORES * span), BF16)] * places,
        in_specs=[VMEM] * 2 + [ANY] * len(after),
        out_specs=[VMEM] * places,
        name="join",
        **params(8),
    )(kept, crossed, *after)


def cross_kernel(places, *refs):
    blocks, out = refs[:places], refs[-1]
    other = 1 - lax.rem(lax.axis_index("mem"), CORES)
    span = (blocks[0].shape[1] - LANES) // CORES
    for step, block in enumerate(blocks):
        out[step, :, pl.ds(0, span)] = block[:, pl.ds(pl.multiple_of(other * span, LANES), span)]
        out[step, :, pl.ds(span, LANES)] = block[:, pl.ds(CORES * span, LANES)]


def cross(blocks, after):
    span = (blocks[0].shape[1] - LANES) // CORES
    return pl.pallas_call(
        functools.partial(cross_kernel, len(blocks)),
        out_shape=jax.ShapeDtypeStruct((len(blocks), ROWS, span + LANES), BF16),
        in_specs=[VMEM] * len(blocks) + [ANY] * len(after),
        out_specs=VMEM,
        name="cross",
        **params(8),
    )(*blocks, *after)


def table_kernel(turns, table, pieces, weights, ctf, square, sem):
    cols = ctf.shape[1]
    start = 0
    if table.shape[1] != cols:
        start = pl.multiple_of(lax.axis_index("mem") * cols, LANES)
    copy = pltpu.make_async_copy(table.at[:, pl.ds(start, cols)], ctf, sem)
    copy.start()
    copy.wait()
    value = ctf[...]
    high = value.astype(BF16).astype(F32)
    mid = (value - high).astype(BF16).astype(F32)
    low = value - high - mid
    stacked = jnp.concatenate([high, mid, low], axis=0).astype(BF16)
    eye = identity()
    pick = (
        lax.broadcasted_iota(jnp.int32, (PIECES * BINS, LANES), 0) % BINS
        == lax.broadcasted_iota(jnp.int32, (PIECES * BINS, LANES), 1) % BINS
    ).astype(BF16)
    for tile in range(cols // LANES):
        rows = pl.ds(tile * LANES, LANES)
        flipped = lax.dot_general(
            eye, stacked[:, tile * LANES : (tile + 1) * LANES], NT, preferred_element_type=F32
        ).astype(BF16)
        pieces[rows, :] = flipped
        spread = jnp.dot(flipped, pick, preferred_element_type=F32)
        square[rows, :] = spread * spread
    turn = lax.broadcasted_iota(jnp.int32, (1, LANES), 1) // BINS
    levels = max(NEAR - 1, 1).bit_length()

    def one(q, carry):
        rows = pl.ds(pl.multiple_of(q * ANGLES, 2 * ROWS), ANGLES)
        block = square[rows, :]
        for level in range(levels):
            chosen = (turn >> level & 1) == 1
            block = jnp.where(chosen, turned(block, SHIFT << level), block)
        high, low = split(block)
        weights[rows, pl.ds(0, LANES)] = high
        weights[rows, pl.ds(LANES, LANES)] = low
        return carry

    lax.fori_loop(0, turns, one, 0, unroll=2)


def tables(table, cols, turns):
    return pl.pallas_call(
        functools.partial(table_kernel, turns),
        out_shape=[
            jax.ShapeDtypeStruct((cols, PIECES * BINS), BF16),
            jax.ShapeDtypeStruct((turns * ANGLES, 2 * LANES), BF16),
        ],
        in_specs=[HBM],
        out_specs=[VMEM, VMEM],
        scratch_shapes=[
            pltpu.VMEM((BINS, cols), F32),
            pltpu.VMEM((cols, LANES), F32),
            pltpu.SemaphoreType.DMA,
        ],
        name="tables",
        **params(8),
    )(table)


def stacked(span):
    return [(low // LANES, min(LANES, span - low)) for low in range(0, span, LANES)]


def sum_rows(span, lanes):
    used = CPG * len(stacked(span)) + 3 * lanes // LANES
    return -(-used // ROWS) * ROWS


def tag_block(message, span):
    low = CPG * len(stacked(span)) // ROWS * ROWS
    return message[low:].astype(F32)


def read_tags(ref, span, lanes):
    rows = CPG * len(stacked(span))
    parts = lanes // LANES
    low = rows - rows // ROWS * ROWS
    return [
        jnp.concatenate([ref[pl.ds(low + kind * parts + part, 1), :] for part in range(parts)], axis=1)
        for kind in range(3)
    ]


def numer_kernel(mem, count, first, rows, base, tiles, segments, pieces, *refs):
    refs = list(refs)
    grp = lax.axis_size("grp")
    lanes = mem * count
    groups = count // ROWS
    places = mem // CORES
    core = lax.rem(lax.axis_index("mem"), CORES)
    own = lax.axis_index("grp")
    if not first:
        tags = refs.pop(0)
    for chunk, wide, src, dst, width in segments:
        across = pl.ds(dst * LANES, width * LANES)
        msgs, refs = refs[:places], refs[places:]
        if chunk == 0:
            crossed = refs.pop(0)
            past = groups * wide * LANES
        for step in range(places):
            for g in range(groups):
                low = (g * wide + src) * LANES
                if chunk == 0:
                    kept = pl.multiple_of(core * (groups * wide * LANES) + low, LANES)
                    near = msgs[step][:, pl.ds(kept, width * LANES)]
                    far = crossed[step, :, pl.ds(low, width * LANES)]
                else:
                    near = msgs[step][:, pl.ds(low, width * LANES)]
                    far = msgs[step][:, pl.ds(groups * wide * LANES + low, width * LANES)]
                refs[-3][pl.ds(step * count + g * ROWS, ROWS), across] = near
                refs[-3][pl.ds((places + step) * count + g * ROWS, ROWS), across] = far
    if first:
        tags = refs.pop(0)
        per_tile = LANES // count
        for tile in range(lanes // LANES):
            total = jnp.zeros((ROWS, LANES), F32)
            for slot in range(tile * per_tile, (tile + 1) * per_tile):
                if slot < places:
                    total += msgs[slot][:, pl.ds(CORES * past, LANES)].astype(F32)
                else:
                    total += crossed[slot - places, :, pl.ds(past, LANES)].astype(F32)
            tags[:, pl.ds(tile * LANES, LANES)] = total
    sums = refs[:grp]
    data, product, parts = refs[grp:]
    label = tags[...].astype(jnp.int32)
    key = label[0:1] * CPAD + label[1:2]
    spot = label[2:3]
    turn = label[3:4]
    pick = (
        lax.broadcasted_iota(jnp.int32, (PIECES * BINS, lanes), 0) % BINS == spot
    ).astype(BF16)
    klass = lax.broadcasted_iota(jnp.int32, (CPAD, lanes), 0)
    member = []
    for step in range(grp):
        one = (klass + CPAD * partner(own, step, grp) == key).astype(BF16)
        member.append(jnp.concatenate([one, one], axis=1))
    eye = identity()
    for tile in range(tiles):
        across = pl.ds(tile * LANES, LANES)
        flipped = lax.dot_general(eye, data[:, across], NT, preferred_element_type=F32)
        ctf = jnp.dot(
            pieces[pl.ds((base + tile) * LANES, LANES), :], pick, preferred_element_type=F32
        )
        product[across, :] = flipped * ctf
    offset = rows[0] * ANGLES - base * LANES

    def rotate(q, carry):
        for tile in range(lanes // LANES):
            block = product[
                pl.ds(pl.multiple_of(offset + q * ANGLES, ROWS), ANGLES),
                pl.ds(tile * LANES, LANES),
            ]
            bits = turn[:, tile * LANES : (tile + 1) * LANES]
            for level in range(LEVELS):
                chosen = (bits >> level & 1) == 1
                block = jnp.where(chosen, turned(block, SHIFT << level), block)
            high, low = split(block)
            where = pl.ds(pl.multiple_of(q * ANGLES, 2 * ROWS), ANGLES)
            parts[where, pl.ds(tile * LANES, LANES)] = high
            parts[where, pl.ds(lanes + tile * LANES, LANES)] = low
        return carry

    lax.fori_loop(0, rows[1] - rows[0], rotate, 0)
    result = lax.dot_general(
        jnp.concatenate(member, axis=0), parts[...], NT, preferred_element_type=F32
    )
    for step in range(grp):
        for tile, width in stacked(result.shape[1]):
            here = (pl.ds(tile * CPG, CPG), pl.ds(0, width))
            value = result[step * CPAD : step * CPAD + CPG, tile * LANES : tile * LANES + width]
            sums[step][here] = value
        if first:
            target = partner(own, step, grp)
            local = jnp.where(label[0:1] == target, label[1:2], -1)
            row = CPG * len(stacked(result.shape[1]))
            for kind in (local, spot, turn):
                for tile in range(lanes // LANES):
                    value = kind[:, tile * LANES : (tile + 1) * LANES].astype(F32)
                    sums[step][pl.ds(row, 1), :] = value
                    row += 1


def numerators(count, pieces, tags, arrived, chunk, edges, rows):
    mem, grp = lax.axis_size("mem"), lax.axis_size("grp")
    first = chunk == 0
    here = (rows[chunk], rows[chunk + 1])
    base = here[0] * ANGLES // LANES
    stop = min(-(-here[1] * ANGLES // LANES), edges[-1])
    segments, msgs = [], []
    for c in range(chunk + 1):
        low, high = max(edges[c], base), min(edges[c + 1], stop)
        if low < high:
            segments.append((c, edges[c + 1] - edges[c], low - edges[c], low - base, high - low))
            msgs += arrived[c]
    lanes = mem * count
    span = (here[1] - here[0]) * ANGLES
    tiles = stop - base
    shapes = [jax.ShapeDtypeStruct((ROWS, lanes), F32)] if first else []
    tall = sum_rows(span, lanes if first else 0)
    shapes += [jax.ShapeDtypeStruct((tall, LANES), F32)] * grp
    operands = [pieces] + ([] if first else [tags]) + msgs
    outs = pl.pallas_call(
        functools.partial(numer_kernel, mem, count, first, here, base, tiles, tuple(segments)),
        out_shape=shapes,
        in_specs=[VMEM] * len(operands),
        out_specs=[VMEM] * len(shapes),
        scratch_shapes=[
            pltpu.VMEM((lanes, tiles * LANES), BF16),
            pltpu.VMEM((tiles * LANES, lanes), F32),
            pltpu.VMEM((span, 2 * lanes), BF16),
        ],
        name="numerators",
        **params(16),
    )(*operands)
    if first:
        return outs[0], outs[1:]
    return tags, outs


def denom_kernel(first, lanes, weights, *refs):
    blocks, (denom, spread) = refs[:-2], refs[-2:]
    span = weights.shape[0]
    klass = lax.broadcasted_iota(jnp.int32, (CPAD, lanes), 0)
    pair = lax.broadcasted_iota(jnp.int32, (PAIRS, lanes), 0)
    count = jnp.zeros((CPAD, PAIRS), F32)
    for ref in blocks:
        local, spot, turn = [label.astype(jnp.int32) for label in read_tags(ref, first, lanes)]
        member = (klass == local).astype(BF16)
        which = (pair == turn * BINS + spot).astype(BF16)
        count += lax.dot_general(member, which, NT, preferred_element_type=F32)
    high, low = split(count)
    left = jnp.concatenate(
        [jnp.concatenate([high, high], axis=1), jnp.concatenate([low, low], axis=1)], axis=0
    )

    def turn_far(q, carry):
        rows = pl.ds(pl.multiple_of(q * ANGLES, 2 * ROWS), ANGLES)
        block = weights[rows, :]
        for tile in range(PAIRS // LANES):
            far = turned(block, SHIFT * NEAR * tile)
            spread[rows, pl.ds(tile * LANES, LANES)] = far[:, :LANES]
            spread[rows, pl.ds(PAIRS + tile * LANES, LANES)] = far[:, LANES:]
        return carry

    lax.fori_loop(0, span // ANGLES, turn_far, 0)
    both = lax.dot_general(left, spread[...], NT, preferred_element_type=F32)
    denom[...] = both[:CPAD] + both[CPAD:]


def denominators(weights, blocks, first, lanes):
    span = weights.shape[0]
    return pl.pallas_call(
        functools.partial(denom_kernel, first, lanes),
        out_shape=jax.ShapeDtypeStruct((CPAD, span), F32),
        in_specs=[VMEM] * (1 + len(blocks)),
        out_specs=VMEM,
        scratch_shapes=[pltpu.VMEM((span, 2 * PAIRS), BF16)],
        name="denominators",
        **params(20),
    )(weights, *blocks)


def average_kernel(rows, denom, *refs):
    sums, out = refs[:-1], refs[-1]
    for chunk in range(len(rows) - 1):
        for tile, width in stacked((rows[chunk + 1] - rows[chunk]) * ANGLES):
            across = pl.ds(rows[chunk] * ANGLES + tile * LANES, width)
            total = sums[chunk][pl.ds(tile * CPG, CPG), pl.ds(0, width)]
            out[:, across] = total / (denom[:CPG, across] + wiener_term)


def averages(denom, sums, rows):
    span = denom.shape[1]
    return pl.pallas_call(
        functools.partial(average_kernel, rows),
        out_shape=jax.ShapeDtypeStruct((CPG, span), F32),
        in_specs=[VMEM] * (1 + len(sums)),
        out_specs=VMEM,
        name="averages",
        **params(8),
    )(denom, *sums)


def plan(span):
    turns = span // ANGLES
    tiles = -(-span // LANES)
    edges = [0, tiles // 2, tiles] if tiles % 2 == 0 else [0, tiles]
    rows = [min(edge * LANES // ANGLES, turns) for edge in edges]
    return tuple(edges), tuple(rows)


def on_device(images, classes, rotations, bins, ctf_table):
    mem, grp = lax.axis_size("mem"), lax.axis_size("grp")
    count = images.shape[0]
    span = images.shape[1] // mem
    edges, rows = plan(span)
    cols = edges[-1] * LANES
    places = mem // CORES
    table = ctf_table
    if cols != span:
        images = jnp.pad(images.reshape(count, mem, span), ((0, 0), (0, 0), (0, cols - span)))
        images = images.reshape(count, mem * cols)
        table = lax.dynamic_slice_in_dim(ctf_table, lax.axis_index("mem") * span, span, 1)
        table = jnp.pad(table, ((0, 0), (0, cols - span)))
    pieces, weights = tables(table, cols, span // ANGLES)
    firsts, seconds = pack(images, jnp.stack([classes, bins, rotations]), cols, edges)
    others = range(places - 1, 0, -1)
    here = {step: send(firsts[step], "mem", step, CORES) for step in others}
    here[0] = firsts[0]
    first = [here[step] for step in range(places)]
    arrived, after = [], [pieces]
    if seconds:
        kept, crossed = seconds[0], send(seconds[1], "mem", 0, CORES, 1)
        msgs = join(kept, crossed, [first[-1], pieces])
        here = {step: send(msgs[step], "mem", step, CORES) for step in others}
        here[0] = msgs[0]
        arrived, after = [[here[step] for step in range(places)]], [msgs[0]]
    arrived = [first + [send(cross(first, after), "mem", 0, CORES, 1)]] + arrived
    tags, sums, blocks = None, [], []
    for chunk in range(len(edges) - 1):
        tags, here = numerators(count, pieces, tags, arrived, chunk, edges, rows)
        others = [send(here[step].astype(HALF), "grp", step) for step in range(1, grp)]
        if chunk == 0:
            blocks = [tag_block(part, rows[1] * ANGLES) for part in [here[0]] + others]
        total = here[0]
        for part in others:
            total = total + part.astype(F32)
        sums.append(total)
    denom = denominators(weights, blocks, rows[1] * ANGLES, mem * count)
    return averages(denom, sums, rows)


def solution(mesh):
    in_specs = (
        P(("grp", "mem"), None),
        P(("grp", "mem")),
        P(("grp", "mem")),
        P(("grp", "mem")),
        P(),
    )
    out_specs = P("grp", "mem")
    return jax.shard_map(
        on_device, mesh=mesh, in_specs=in_specs, out_specs=out_specs, check_vma=False
    )
```

```python
import functools

import jax
import jax.numpy as jnp
from jax import lax
from jax.experimental import pallas as pl
from jax.experimental.pallas import tpu as pltpu
from jax.sharding import PartitionSpec as P

ANGLES = 144
ROTS = 36
BINS = 16
CPG = 50
SHIFT = 4

LANES = 128
ROWS = 8
CORES = 2
CPAD = -(-CPG // ROWS) * ROWS
PIECES = 3
NEAR = LANES // BINS
PAIRS = -(-ROTS // NEAR) * LANES
LEVELS = max(ROTS - 1, 1).bit_length()

wiener_term = 1.0

F32 = jnp.float32
BF16 = jnp.bfloat16
HALF = jnp.float16
NT = (((1,), (1,)), ((), ()))
ANY = pl.BlockSpec(memory_space=pl.ANY)
HBM = pl.BlockSpec(memory_space=pltpu.HBM)
VMEM = pl.BlockSpec(memory_space=pltpu.VMEM)


def partner(index, step, size):
    if size & (size - 1) == 0:
        return index ^ step
    return lax.rem(index + step, size) if not isinstance(index, int) else (index + step) % size


def send(value, axis, step, cores=1, cross=0):
    size = lax.axis_size(axis) // cores
    pairs = [
        (i * cores + core, partner(i, step, size) * cores + (core ^ cross))
        for i in range(size)
        for core in range(cores)
    ]
    return lax.ppermute(value, axis, pairs)


def identity():
    rows = lax.broadcasted_iota(jnp.int32, (LANES, LANES), 0)
    cols = lax.broadcasted_iota(jnp.int32, (LANES, LANES), 1)
    return (rows == cols).astype(BF16)


def turned(block, amount):
    amount %= ANGLES
    if amount == 0:
        return block
    if amount % ROWS == 0:
        return jnp.concatenate([block[amount:], block[:amount]], axis=0)
    return pltpu.roll(block, ANGLES - amount, 0)


def split(value):
    high = value.astype(BF16)
    low = (value - high.astype(F32)).astype(BF16)
    return high, low


def params(mebibytes):
    return dict(
        compiler_params=pltpu.CompilerParams(vmem_limit_bytes=mebibytes << 20),
        cost_estimate=pl.CostEstimate(flops=1 << 20, bytes_accessed=1 << 16, transcendentals=0),
    )


def pack_kernel(mem, cols, edges, img, labels, *outs):
    places = mem // CORES
    count = img.shape[0]
    groups = count // ROWS
    here = lax.axis_index("mem") // CORES
    core = lax.rem(lax.axis_index("mem"), CORES)
    label = labels[0:1]
    owner = jnp.zeros_like(label)
    for g in range(1, lax.axis_size("grp")):
        owner += (label >= g * CPG).astype(jnp.int32)
    row = lax.broadcasted_iota(jnp.int32, (ROWS, count), 0) % (ROWS // CORES)
    stack = jnp.where(
        row == 0,
        owner,
        jnp.where(
            row == 1,
            label - owner * CPG,
            jnp.where(row == 2, labels[1:2], jnp.where(row == 3, labels[2:3], 0)),
        ),
    )
    spread = (
        lax.broadcasted_iota(jnp.int32, (count, LANES), 1) % count
        == lax.broadcasted_iota(jnp.int32, (count, LANES), 0)
    ).astype(BF16)
    tags = jnp.dot(stack.astype(F32).astype(BF16), spread, preferred_element_type=F32)
    place = lax.broadcasted_iota(jnp.int32, (ROWS, LANES), 1) // count
    lower = lax.broadcasted_iota(jnp.int32, (ROWS, LANES), 0) // (ROWS // CORES)
    first = (edges[1] - edges[0]) * LANES
    for step in range(places):
        there = partner(here, step, places) * CORES
        for target in range(CORES):
            start = pl.multiple_of((there + target) * cols + edges[0] * LANES, LANES)
            for g in range(groups):
                outs[step][:, pl.ds((target * groups + g) * first, first)] = img[
                    pl.ds(g * ROWS, ROWS), pl.ds(start, first)
                ]
        slot = (step * CORES + lower) % (LANES // count)
        mine = jnp.where(place == slot, tags, 0.0)
        outs[step][:, pl.ds(CORES * groups * first, LANES)] = mine.astype(BF16)
        if len(edges) == 2:
            continue
        width = (edges[2] - edges[1]) * LANES
        for cross in range(CORES):
            start = pl.multiple_of((there + (core ^ cross)) * cols + edges[1] * LANES, LANES)
            for g in range(groups):
                outs[places + cross][step, :, pl.ds(g * width, width)] = img[
                    pl.ds(g * ROWS, ROWS), pl.ds(start, width)
                ]


def pack(images, labels, cols, edges):
    mem = lax.axis_size("mem")
    groups = images.shape[0] // ROWS
    wide = [groups * (high - low) * LANES for low, high in zip(edges, edges[1:])]
    shapes = [jax.ShapeDtypeStruct((ROWS, CORES * wide[0] + LANES), BF16)] * (mem // CORES)
    for width in wide[1:]:
        shapes += [jax.ShapeDtypeStruct((mem // CORES, ROWS, width), BF16)] * CORES
    outs = pl.pallas_call(
        functools.partial(pack_kernel, mem, cols, edges),
        out_shape=shapes,
        in_specs=[VMEM] * 2,
        out_specs=[VMEM] * len(shapes),
        name="pack",
        **params(8),
    )(images, labels)
    return outs[: mem // CORES], outs[mem // CORES :]


def join_kernel(kept, crossed, *refs):
    places, _, span = kept.shape
    outs = refs[-places:]
    for step in range(places):
        outs[step][:, pl.ds(0, span)] = kept[step]
        outs[step][:, pl.ds(span, span)] = crossed[step]


def join(kept, crossed, after):
    places, _, span = kept.shape
    return pl.pallas_call(
        join_kernel,
        out_shape=[jax.ShapeDtypeStruct((ROWS, CORES * span), BF16)] * places,
        in_specs=[VMEM] * 2 + [ANY] * len(after),
        out_specs=[VMEM] * places,
        name="join",
        **params(8),
    )(kept, crossed, *after)


def cross_kernel(places, *refs):
    blocks, out = refs[:places], refs[-1]
    other = 1 - lax.rem(lax.axis_index("mem"), CORES)
    span = (blocks[0].shape[1] - LANES) // CORES
    for step, block in enumerate(blocks):
        out[step, :, pl.ds(0, span)] = block[:, pl.ds(pl.multiple_of(other * span, LANES), span)]
        out[step, :, pl.ds(span, LANES)] = block[:, pl.ds(CORES * span, LANES)]


def cross(blocks, after):
    span = (blocks[0].shape[1] - LANES) // CORES
    return pl.pallas_call(
        functools.partial(cross_kernel, len(blocks)),
        out_shape=jax.ShapeDtypeStruct((len(blocks), ROWS, span + LANES), BF16),
        in_specs=[VMEM] * len(blocks) + [ANY] * len(after),
        out_specs=VMEM,
        name="cross",
        **params(8),
    )(*blocks, *after)


def table_kernel(turns, table, pieces, weights, ctf, square, sem):
    cols = ctf.shape[1]
    start = 0
    if table.shape[1] != cols:
        start = pl.multiple_of(lax.axis_index("mem") * cols, LANES)
    copy = pltpu.make_async_copy(table.at[:, pl.ds(start, cols)], ctf, sem)
    copy.start()
    copy.wait()
    value = ctf[...]
    high = value.astype(BF16).astype(F32)
    mid = (value - high).astype(BF16).astype(F32)
    low = value - high - mid
    stacked = jnp.concatenate([high, mid, low], axis=0).astype(BF16)
    eye = identity()
    pick = (
        lax.broadcasted_iota(jnp.int32, (PIECES * BINS, LANES), 0) % BINS
        == lax.broadcasted_iota(jnp.int32, (PIECES * BINS, LANES), 1) % BINS
    ).astype(BF16)
    for tile in range(cols // LANES):
        rows = pl.ds(tile * LANES, LANES)
        flipped = lax.dot_general(
            eye, stacked[:, tile * LANES : (tile + 1) * LANES], NT, preferred_element_type=F32
        ).astype(BF16)
        pieces[rows, :] = flipped
        spread = jnp.dot(flipped, pick, preferred_element_type=F32)
        square[rows, :] = spread * spread
    turn = lax.broadcasted_iota(jnp.int32, (1, LANES), 1) // BINS
    levels = max(NEAR - 1, 1).bit_length()

    def one(q, carry):
        rows = pl.ds(pl.multiple_of(q * ANGLES, 2 * ROWS), ANGLES)
        block = square[rows, :]
        for level in range(levels):
            chosen = (turn >> level & 1) == 1
            block = jnp.where(chosen, turned(block, SHIFT << level), block)
        high, low = split(block)
        weights[rows, pl.ds(0, LANES)] = high
        weights[rows, pl.ds(LANES, LANES)] = low
        return carry

    lax.fori_loop(0, turns, one, 0, unroll=2)


def tables(table, cols, turns):
    return pl.pallas_call(
        functools.partial(table_kernel, turns),
        out_shape=[
            jax.ShapeDtypeStruct((cols, PIECES * BINS), BF16),
            jax.ShapeDtypeStruct((turns * ANGLES, 2 * LANES), BF16),
        ],
        in_specs=[HBM],
        out_specs=[VMEM, VMEM],
        scratch_shapes=[
            pltpu.VMEM((BINS, cols), F32),
            pltpu.VMEM((cols, LANES), F32),
            pltpu.SemaphoreType.DMA,
        ],
        name="tables",
        **params(8),
    )(table)


def stacked(span):
    return [(low // LANES, min(LANES, span - low)) for low in range(0, span, LANES)]


def sum_rows(span, lanes):
    used = CPG * len(stacked(span)) + 3 * lanes // LANES
    return -(-used // ROWS) * ROWS


def tag_block(message, span):
    low = CPG * len(stacked(span)) // ROWS * ROWS
    return message[low:].astype(F32)


def read_tags(ref, span, lanes):
    rows = CPG * len(stacked(span))
    parts = lanes // LANES
    low = rows - rows // ROWS * ROWS
    return [
        jnp.concatenate([ref[pl.ds(low + kind * parts + part, 1), :] for part in range(parts)], axis=1)
        for kind in range(3)
    ]


def numer_kernel(mem, count, first, rows, base, tiles, segments, steps, added, pieces, *refs):
    refs = list(refs)
    grp = lax.axis_size("grp")
    lanes = (steps[1] - steps[0]) * CORES * count
    groups = count // ROWS
    places = mem // CORES
    core = lax.rem(lax.axis_index("mem"), CORES)
    own = lax.axis_index("grp")
    if not first:
        tags = refs.pop(0)
    for chunk, wide, src, dst, width in segments:
        across = pl.ds(dst * LANES, width * LANES)
        taken = places if chunk == 0 else steps[1] - steps[0]
        msgs, refs = refs[:taken], refs[taken:]
        if chunk == 0:
            crossed = refs.pop(0)
            past = groups * wide * LANES
        for step in range(*steps):
            for g in range(groups):
                low = (g * wide + src) * LANES
                if chunk == 0:
                    kept = pl.multiple_of(core * (groups * wide * LANES) + low, LANES)
                    near = msgs[step][:, pl.ds(kept, width * LANES)]
                    far = crossed[step, :, pl.ds(low, width * LANES)]
                else:
                    msg = msgs[step - steps[0]]
                    near = msg[:, pl.ds(low, width * LANES)]
                    far = msg[:, pl.ds(groups * wide * LANES + low, width * LANES)]
                at = (step - steps[0]) * CORES * count + g * ROWS
                refs[-3][pl.ds(at, ROWS), across] = near
                refs[-3][pl.ds(at + count, ROWS), across] = far
    partial = refs[:added]
    refs = refs[added:]
    if first:
        tags = refs.pop(0)
        per_tile = LANES // count
        half = ROWS // CORES
        for tile in range(lanes // LANES):
            total = jnp.zeros((ROWS, LANES), F32)
            for slot in range(tile * per_tile, (tile + 1) * per_tile, CORES):
                step = slot // CORES
                near = msgs[step][:, pl.ds(CORES * past, LANES)].astype(F32)
                far = crossed[step, :, pl.ds(past, LANES)].astype(F32)
                total += jnp.concatenate([near[:half] + far[half:], near[half:]], axis=0)
            tags[:, pl.ds(tile * LANES, LANES)] = total
    sums = refs[:grp]
    data, product, parts = refs[grp:]
    label = tags[:, pl.ds(steps[0] * CORES * count, lanes)].astype(jnp.int32)
    key = label[0:1] * CPAD + label[1:2]
    spot = label[2:3]
    turn = label[3:4]
    pick = (
        lax.broadcasted_iota(jnp.int32, (PIECES * BINS, lanes), 0) % BINS == spot
    ).astype(BF16)
    klass = lax.broadcasted_iota(jnp.int32, (CPAD, lanes), 0)
    member = []
    for step in range(grp):
        one = (klass + CPAD * partner(own, step, grp) == key).astype(BF16)
        member.append(jnp.concatenate([one, one], axis=1))
    eye = identity()
    for tile in range(tiles):
        across = pl.ds(tile * LANES, LANES)
        flipped = lax.dot_general(eye, data[:, across], NT, preferred_element_type=F32)
        ctf = jnp.dot(
            pieces[pl.ds((base + tile) * LANES, LANES), :], pick, preferred_element_type=F32
        )
        product[across, :] = flipped * ctf
    offset = rows[0] * ANGLES - base * LANES

    def rotate(q, carry):
        for tile in range(lanes // LANES):
            block = product[
                pl.ds(pl.multiple_of(offset + q * ANGLES, ROWS), ANGLES),
                pl.ds(tile * LANES, LANES),
            ]
            bits = turn[:, tile * LANES : (tile + 1) * LANES]
            for level in range(LEVELS):
                chosen = (bits >> level & 1) == 1
                block = jnp.where(chosen, turned(block, SHIFT << level), block)
            high, low = split(block)
            where = pl.ds(pl.multiple_of(q * ANGLES, 2 * ROWS), ANGLES)
            parts[where, pl.ds(tile * LANES, LANES)] = high
            parts[where, pl.ds(lanes + tile * LANES, LANES)] = low
        return carry

    lax.fori_loop(0, rows[1] - rows[0], rotate, 0)
    result = lax.dot_general(
        jnp.concatenate(member, axis=0), parts[...], NT, preferred_element_type=F32
    )
    for step in range(grp):
        for tile, width in stacked(result.shape[1]):
            here = (pl.ds(tile * CPG, CPG), pl.ds(0, width))
            value = result[step * CPAD : step * CPAD + CPG, tile * LANES : tile * LANES + width]
            sums[step][here] = value + partial[step][here] if partial else value
        if first:
            target = partner(own, step, grp)
            local = jnp.where(label[0:1] == target, label[1:2], -1)
            row = CPG * len(stacked(result.shape[1]))
            for kind in (local, spot, turn):
                for tile in range(lanes // LANES):
                    value = kind[:, tile * LANES : (tile + 1) * LANES].astype(F32)
                    sums[step][pl.ds(row, 1), :] = value
                    row += 1


def numerators(count, pieces, tags, arrived, chunk, edges, rows, steps, partial=()):
    mem, grp = lax.axis_size("mem"), lax.axis_size("grp")
    first = chunk == 0
    here = (rows[chunk], rows[chunk + 1])
    base = here[0] * ANGLES // LANES
    stop = min(-(-here[1] * ANGLES // LANES), edges[-1])
    segments, msgs = [], []
    for c in range(chunk + 1):
        low, high = max(edges[c], base), min(edges[c + 1], stop)
        if low < high:
            segments.append((c, edges[c + 1] - edges[c], low - edges[c], low - base, high - low))
            msgs += arrived[c] if c == 0 else arrived[c][slice(*steps)]
    lanes = (steps[1] - steps[0]) * CORES * count
    span = (here[1] - here[0]) * ANGLES
    tiles = stop - base
    shapes = [jax.ShapeDtypeStruct((ROWS, lanes), F32)] if first else []
    tall = sum_rows(span, lanes if first else 0)
    shapes += [jax.ShapeDtypeStruct((tall, LANES), F32)] * grp
    operands = [pieces] + ([] if first else [tags]) + msgs + list(partial)
    outs = pl.pallas_call(
        functools.partial(
            numer_kernel, mem, count, first, here, base, tiles, tuple(segments), steps, len(partial)
        ),
        out_shape=shapes,
        in_specs=[VMEM] * len(operands),
        out_specs=[VMEM] * len(shapes),
        scratch_shapes=[
            pltpu.VMEM((lanes, tiles * LANES), BF16),
            pltpu.VMEM((tiles * LANES, lanes), F32),
            pltpu.VMEM((span, 2 * lanes), BF16),
        ],
        name="numerators",
        **params(16),
    )(*operands)
    if first:
        return outs[0], outs[1:]
    return tags, outs


def denom_kernel(first, lanes, weights, *refs):
    blocks, (denom, spread) = refs[:-2], refs[-2:]
    span = weights.shape[0]
    klass = lax.broadcasted_iota(jnp.int32, (CPAD, lanes), 0)
    pair = lax.broadcasted_iota(jnp.int32, (PAIRS, lanes), 0)
    count = jnp.zeros((CPAD, PAIRS), F32)
    for ref in blocks:
        local, spot, turn = [label.astype(jnp.int32) for label in read_tags(ref, first, lanes)]
        member = (klass == local).astype(BF16)
        which = (pair == turn * BINS + spot).astype(BF16)
        count += lax.dot_general(member, which, NT, preferred_element_type=F32)
    high, low = split(count)
    left = jnp.concatenate(
        [jnp.concatenate([high, high], axis=1), jnp.concatenate([low, low], axis=1)], axis=0
    )

    def turn_far(q, carry):
        rows = pl.ds(pl.multiple_of(q * ANGLES, 2 * ROWS), ANGLES)
        block = weights[rows, :]
        for tile in range(PAIRS // LANES):
            far = turned(block, SHIFT * NEAR * tile)
            spread[rows, pl.ds(tile * LANES, LANES)] = far[:, :LANES]
            spread[rows, pl.ds(PAIRS + tile * LANES, LANES)] = far[:, LANES:]
        return carry

    lax.fori_loop(0, span // ANGLES, turn_far, 0)
    both = lax.dot_general(left, spread[...], NT, preferred_element_type=F32)
    denom[...] = both[:CPAD] + both[CPAD:]


def denominators(weights, blocks, first, lanes):
    span = weights.shape[0]
    return pl.pallas_call(
        functools.partial(denom_kernel, first, lanes),
        out_shape=jax.ShapeDtypeStruct((CPAD, span), F32),
        in_specs=[VMEM] * (1 + len(blocks)),
        out_specs=VMEM,
        scratch_shapes=[pltpu.VMEM((span, 2 * PAIRS), BF16)],
        name="denominators",
        **params(20),
    )(weights, *blocks)


def average_kernel(rows, denom, *refs):
    sums, out = refs[:-1], refs[-1]
    for chunk in range(len(rows) - 1):
        for tile, width in stacked((rows[chunk + 1] - rows[chunk]) * ANGLES):
            across = pl.ds(rows[chunk] * ANGLES + tile * LANES, width)
            total = sums[chunk][pl.ds(tile * CPG, CPG), pl.ds(0, width)]
            out[:, across] = total / (denom[:CPG, across] + wiener_term)


def averages(denom, sums, rows):
    span = denom.shape[1]
    return pl.pallas_call(
        functools.partial(average_kernel, rows),
        out_shape=jax.ShapeDtypeStruct((CPG, span), F32),
        in_specs=[VMEM] * (1 + len(sums)),
        out_specs=VMEM,
        name="averages",
        **params(8),
    )(denom, *sums)


def plan(span):
    turns = span // ANGLES
    tiles = -(-span // LANES)
    edges = [0, tiles // 2, tiles] if tiles % 2 == 0 else [0, tiles]
    rows = [min(edge * LANES // ANGLES, turns) for edge in edges]
    return tuple(edges), tuple(rows)


def on_device(images, classes, rotations, bins, ctf_table):
    mem, grp = lax.axis_size("mem"), lax.axis_size("grp")
    count = images.shape[0]
    span = images.shape[1] // mem
    edges, rows = plan(span)
    cols = edges[-1] * LANES
    places = mem // CORES
    table = ctf_table
    if cols != span:
        images = jnp.pad(images.reshape(count, mem, span), ((0, 0), (0, 0), (0, cols - span)))
        images = images.reshape(count, mem * cols)
        table = lax.dynamic_slice_in_dim(ctf_table, lax.axis_index("mem") * span, span, 1)
        table = jnp.pad(table, ((0, 0), (0, cols - span)))
    pieces, weights = tables(table, cols, span // ANGLES)
    firsts, seconds = pack(images, jnp.stack([classes, bins, rotations]), cols, edges)
    others = range(places - 1, 0, -1)
    here = {step: send(firsts[step], "mem", step, CORES) for step in others}
    here[0] = firsts[0]
    first = [here[step] for step in range(places)]
    arrived, after = [], [pieces]
    if seconds:
        kept, crossed = seconds[0], send(seconds[1], "mem", 0, CORES, 1)
        msgs = join(kept, crossed, [first[-1], pieces])
        here = {step: send(msgs[step], "mem", step, CORES) for step in others}
        here[0] = msgs[0]
        arrived, after = [[here[step] for step in range(places)]], [msgs[0]]
    arrived = [first + [send(cross(first, after), "mem", 0, CORES, 1)]] + arrived
    tags, sums, blocks = None, [], []
    for chunk in range(len(edges) - 1):
        cuts = [0, places]
        if chunk > 0 and places // 2 * CORES * count % LANES == 0:
            cuts = [0, places // 2, places]
        here = ()
        for steps in zip(cuts, cuts[1:]):
            tags, here = numerators(count, pieces, tags, arrived, chunk, edges, rows, steps, here)
        others = [send(here[step].astype(HALF), "grp", step) for step in range(1, grp)]
        if chunk == 0:
            blocks = [tag_block(part, rows[1] * ANGLES) for part in [here[0]] + others]
        total = here[0]
        for part in others:
            total = total + part.astype(F32)
        sums.append(total)
    denom = denominators(weights, blocks, rows[1] * ANGLES, mem * count)
    return averages(denom, sums, rows)


def solution(mesh):
    in_specs = (
        P(("grp", "mem"), None),
        P(("grp", "mem")),
        P(("grp", "mem")),
        P(("grp", "mem")),
        P(),
    )
    out_specs = P("grp", "mem")
    return jax.shard_map(
        on_device, mesh=mesh, in_specs=in_specs, out_specs=out_specs, check_vma=False
    )
```

```python
import functools

import jax
import jax.numpy as jnp
from jax import lax
from jax.experimental import pallas as pl
from jax.experimental.pallas import tpu as pltpu
from jax.sharding import PartitionSpec as P

ANGLES = 144
ROTS = 36
BINS = 16
CPG = 50
SHIFT = 4

LANES = 128
ROWS = 8
CORES = 2
CPAD = -(-CPG // ROWS) * ROWS
PIECES = 3
NEAR = LANES // BINS
PAIRS = -(-ROTS // NEAR) * LANES
LEVELS = max(ROTS - 1, 1).bit_length()

wiener_term = 1.0

F32 = jnp.float32
BF16 = jnp.bfloat16
HALF = jnp.float16
NT = (((1,), (1,)), ((), ()))
ANY = pl.BlockSpec(memory_space=pl.ANY)
HBM = pl.BlockSpec(memory_space=pltpu.HBM)
VMEM = pl.BlockSpec(memory_space=pltpu.VMEM)


def partner(index, step, size):
    if size & (size - 1) == 0:
        return index ^ step
    return lax.rem(index + step, size) if not isinstance(index, int) else (index + step) % size


def send(value, axis, step, cores=1, cross=0):
    size = lax.axis_size(axis) // cores
    pairs = [
        (i * cores + core, partner(i, step, size) * cores + (core ^ cross))
        for i in range(size)
        for core in range(cores)
    ]
    return lax.ppermute(value, axis, pairs)


def identity():
    rows = lax.broadcasted_iota(jnp.int32, (LANES, LANES), 0)
    cols = lax.broadcasted_iota(jnp.int32, (LANES, LANES), 1)
    return (rows == cols).astype(BF16)


def turned(block, amount):
    amount %= ANGLES
    if amount == 0:
        return block
    if amount % ROWS == 0:
        return jnp.concatenate([block[amount:], block[:amount]], axis=0)
    return pltpu.roll(block, ANGLES - amount, 0)


def split(value):
    high = value.astype(BF16)
    low = (value - high.astype(F32)).astype(BF16)
    return high, low


def params(mebibytes):
    return dict(
        compiler_params=pltpu.CompilerParams(vmem_limit_bytes=mebibytes << 20),
        cost_estimate=pl.CostEstimate(flops=1 << 20, bytes_accessed=1 << 16, transcendentals=0),
    )


def pack_kernel(mem, cols, edges, img, labels, *outs):
    places = mem // CORES
    count = img.shape[0]
    groups = count // ROWS
    here = lax.axis_index("mem") // CORES
    core = lax.rem(lax.axis_index("mem"), CORES)
    label = labels[0:1]
    owner = jnp.zeros_like(label)
    for g in range(1, lax.axis_size("grp")):
        owner += (label >= g * CPG).astype(jnp.int32)
    row = lax.broadcasted_iota(jnp.int32, (ROWS, count), 0) % (ROWS // CORES)
    stack = jnp.where(
        row == 0,
        owner,
        jnp.where(
            row == 1,
            label - owner * CPG,
            jnp.where(row == 2, labels[1:2], jnp.where(row == 3, labels[2:3], 0)),
        ),
    )
    spread = (
        lax.broadcasted_iota(jnp.int32, (count, LANES), 1) % count
        == lax.broadcasted_iota(jnp.int32, (count, LANES), 0)
    ).astype(BF16)
    tags = jnp.dot(stack.astype(F32).astype(BF16), spread, preferred_element_type=F32)
    place = lax.broadcasted_iota(jnp.int32, (ROWS, LANES), 1) // count
    lower = lax.broadcasted_iota(jnp.int32, (ROWS, LANES), 0) // (ROWS // CORES)
    first = (edges[1] - edges[0]) * LANES
    for step in range(places):
        there = partner(here, step, places) * CORES
        for target in range(CORES):
            start = pl.multiple_of((there + target) * cols + edges[0] * LANES, LANES)
            for g in range(groups):
                outs[step][:, pl.ds((target * groups + g) * first, first)] = img[
                    pl.ds(g * ROWS, ROWS), pl.ds(start, first)
                ]
        slot = (step * CORES + lower) % (LANES // count)
        mine = jnp.where(place == slot, tags, 0.0)
        outs[step][:, pl.ds(CORES * groups * first, LANES)] = mine.astype(BF16)
        if len(edges) == 2:
            continue
        width = (edges[2] - edges[1]) * LANES
        for cross in range(CORES):
            start = pl.multiple_of((there + (core ^ cross)) * cols + edges[1] * LANES, LANES)
            for g in range(groups):
                outs[places + cross][step, :, pl.ds(g * width, width)] = img[
                    pl.ds(g * ROWS, ROWS), pl.ds(start, width)
                ]


def pack(images, labels, cols, edges):
    mem = lax.axis_size("mem")
    groups = images.shape[0] // ROWS
    wide = [groups * (high - low) * LANES for low, high in zip(edges, edges[1:])]
    shapes = [jax.ShapeDtypeStruct((ROWS, CORES * wide[0] + LANES), BF16)] * (mem // CORES)
    for width in wide[1:]:
        shapes += [jax.ShapeDtypeStruct((mem // CORES, ROWS, width), BF16)] * CORES
    outs = pl.pallas_call(
        functools.partial(pack_kernel, mem, cols, edges),
        out_shape=shapes,
        in_specs=[VMEM] * 2,
        out_specs=[VMEM] * len(shapes),
        name="pack",
        **params(8),
    )(images, labels)
    return outs[: mem // CORES], outs[mem // CORES :]


def join_kernel(kept, crossed, *refs):
    places, _, span = kept.shape
    outs = refs[-places:]
    for step in range(places):
        outs[step][:, pl.ds(0, span)] = kept[step]
        outs[step][:, pl.ds(span, span)] = crossed[step]


def join(kept, crossed, after):
    places, _, span = kept.shape
    return pl.pallas_call(
        join_kernel,
        out_shape=[jax.ShapeDtypeStruct((ROWS, CORES * span), BF16)] * places,
        in_specs=[VMEM] * 2 + [ANY] * len(after),
        out_specs=[VMEM] * places,
        name="join",
        **params(8),
    )(kept, crossed, *after)


def cross_kernel(places, *refs):
    blocks, out = refs[:places], refs[-1]
    other = 1 - lax.rem(lax.axis_index("mem"), CORES)
    span = (blocks[0].shape[1] - LANES) // CORES
    for step, block in enumerate(blocks):
        out[step, :, pl.ds(0, span)] = block[:, pl.ds(pl.multiple_of(other * span, LANES), span)]
        out[step, :, pl.ds(span, LANES)] = block[:, pl.ds(CORES * span, LANES)]


def cross(blocks, after):
    span = (blocks[0].shape[1] - LANES) // CORES
    return pl.pallas_call(
        functools.partial(cross_kernel, len(blocks)),
        out_shape=jax.ShapeDtypeStruct((len(blocks), ROWS, span + LANES), BF16),
        in_specs=[VMEM] * len(blocks) + [ANY] * len(after),
        out_specs=VMEM,
        name="cross",
        **params(8),
    )(*blocks, *after)


def table_kernel(turns, table, pieces, weights, ctf, square, sem):
    cols = ctf.shape[1]
    start = 0
    if table.shape[1] != cols:
        start = pl.multiple_of(lax.axis_index("mem") * cols, LANES)
    copy = pltpu.make_async_copy(table.at[:, pl.ds(start, cols)], ctf, sem)
    copy.start()
    copy.wait()
    value = ctf[...]
    high = value.astype(BF16).astype(F32)
    mid = (value - high).astype(BF16).astype(F32)
    low = value - high - mid
    stacked = jnp.concatenate([high, mid, low], axis=0).astype(BF16)
    eye = identity()
    pick = (
        lax.broadcasted_iota(jnp.int32, (PIECES * BINS, LANES), 0) % BINS
        == lax.broadcasted_iota(jnp.int32, (PIECES * BINS, LANES), 1) % BINS
    ).astype(BF16)
    for tile in range(cols // LANES):
        rows = pl.ds(tile * LANES, LANES)
        flipped = lax.dot_general(
            eye, stacked[:, tile * LANES : (tile + 1) * LANES], NT, preferred_element_type=F32
        ).astype(BF16)
        pieces[rows, :] = flipped
        spread = jnp.dot(flipped, pick, preferred_element_type=F32)
        square[rows, :] = spread * spread
    turn = lax.broadcasted_iota(jnp.int32, (1, LANES), 1) // BINS
    levels = max(NEAR - 1, 1).bit_length()

    def one(q, carry):
        rows = pl.ds(pl.multiple_of(q * ANGLES, 2 * ROWS), ANGLES)
        block = square[rows, :]
        for level in range(levels):
            chosen = (turn >> level & 1) == 1
            block = jnp.where(chosen, turned(block, SHIFT << level), block)
        high, low = split(block)
        weights[rows, pl.ds(0, LANES)] = high
        weights[rows, pl.ds(LANES, LANES)] = low
        return carry

    lax.fori_loop(0, turns, one, 0, unroll=2)


def tables(table, cols, turns):
    return pl.pallas_call(
        functools.partial(table_kernel, turns),
        out_shape=[
            jax.ShapeDtypeStruct((cols, PIECES * BINS), BF16),
            jax.ShapeDtypeStruct((turns * ANGLES, 2 * LANES), BF16),
        ],
        in_specs=[HBM],
        out_specs=[VMEM, VMEM],
        scratch_shapes=[
            pltpu.VMEM((BINS, cols), F32),
            pltpu.VMEM((cols, LANES), F32),
            pltpu.SemaphoreType.DMA,
        ],
        name="tables",
        **params(8),
    )(table)


def stacked(span):
    return [(low // LANES, min(LANES, span - low)) for low in range(0, span, LANES)]


def sum_rows(span, lanes):
    used = CPG * len(stacked(span)) + 3 * lanes // LANES
    return -(-used // ROWS) * ROWS


def tag_block(message, span):
    low = CPG * len(stacked(span)) // ROWS * ROWS
    return message[low:].astype(F32)


def read_tags(ref, span, lanes):
    rows = CPG * len(stacked(span))
    parts = lanes // LANES
    low = rows - rows // ROWS * ROWS
    return [
        jnp.concatenate([ref[pl.ds(low + kind * parts + part, 1), :] for part in range(parts)], axis=1)
        for kind in range(3)
    ]


def numer_kernel(mem, count, first, rows, base, tiles, segments, steps, added, pieces, *refs):
    refs = list(refs)
    grp = lax.axis_size("grp")
    lanes = (steps[1] - steps[0]) * CORES * count
    groups = count // ROWS
    places = mem // CORES
    core = lax.rem(lax.axis_index("mem"), CORES)
    own = lax.axis_index("grp")
    if not first:
        tags = refs.pop(0)
    for chunk, wide, src, dst, width in segments:
        across = pl.ds(dst * LANES, width * LANES)
        taken = places if chunk == 0 else steps[1] - steps[0]
        msgs, refs = refs[:taken], refs[taken:]
        if chunk == 0:
            crossed = refs.pop(0)
            past = groups * wide * LANES
        for step in range(*steps):
            for g in range(groups):
                low = (g * wide + src) * LANES
                if chunk == 0:
                    kept = pl.multiple_of(core * (groups * wide * LANES) + low, LANES)
                    near = msgs[step][:, pl.ds(kept, width * LANES)]
                    far = crossed[step, :, pl.ds(low, width * LANES)]
                else:
                    msg = msgs[step - steps[0]]
                    near = msg[:, pl.ds(low, width * LANES)]
                    far = msg[:, pl.ds(groups * wide * LANES + low, width * LANES)]
                at = (step - steps[0]) * CORES * count + g * ROWS
                refs[-3][pl.ds(at, ROWS), across] = near
                refs[-3][pl.ds(at + count, ROWS), across] = far
    partial = refs[:added]
    refs = refs[added:]
    if first:
        tags = refs.pop(0)
        per_tile = LANES // count
        half = ROWS // CORES
        for tile in range(lanes // LANES):
            total = jnp.zeros((ROWS, LANES), F32)
            for slot in range(tile * per_tile, (tile + 1) * per_tile, CORES):
                step = slot // CORES
                near = msgs[step][:, pl.ds(CORES * past, LANES)].astype(F32)
                far = crossed[step, :, pl.ds(past, LANES)].astype(F32)
                total += jnp.concatenate([near[:half] + far[half:], near[half:]], axis=0)
            tags[:, pl.ds(tile * LANES, LANES)] = total
    sums = refs[:grp]
    data, product, parts = refs[grp:]
    label = tags[:, pl.ds(steps[0] * CORES * count, lanes)].astype(jnp.int32)
    key = label[0:1] * CPAD + label[1:2]
    spot = label[2:3]
    turn = label[3:4]
    pick = (
        lax.broadcasted_iota(jnp.int32, (PIECES * BINS, lanes), 0) % BINS == spot
    ).astype(BF16)
    klass = lax.broadcasted_iota(jnp.int32, (CPAD, lanes), 0)
    member = []
    for step in range(grp):
        one = (klass + CPAD * partner(own, step, grp) == key).astype(BF16)
        member.append(jnp.concatenate([one, one], axis=1))
    eye = identity()
    for tile in range(tiles):
        across = pl.ds(tile * LANES, LANES)
        flipped = lax.dot_general(eye, data[:, across], NT, preferred_element_type=F32)
        ctf = jnp.dot(
            pieces[pl.ds((base + tile) * LANES, LANES), :], pick, preferred_element_type=F32
        )
        product[across, :] = flipped * ctf
    offset = rows[0] * ANGLES - base * LANES

    def rotate(q, carry):
        for tile in range(lanes // LANES):
            block = product[
                pl.ds(pl.multiple_of(offset + q * ANGLES, ROWS), ANGLES),
                pl.ds(tile * LANES, LANES),
            ]
            bits = turn[:, tile * LANES : (tile + 1) * LANES]
            for level in range(LEVELS):
                chosen = (bits >> level & 1) == 1
                block = jnp.where(chosen, turned(block, SHIFT << level), block)
            high, low = split(block)
            where = pl.ds(pl.multiple_of(q * ANGLES, 2 * ROWS), ANGLES)
            parts[where, pl.ds(tile * LANES, LANES)] = high
            parts[where, pl.ds(lanes + tile * LANES, LANES)] = low
        return carry

    lax.fori_loop(0, rows[1] - rows[0], rotate, 0, unroll=True)
    result = lax.dot_general(
        jnp.concatenate(member, axis=0), parts[...], NT, preferred_element_type=F32
    )
    for step in range(grp):
        for tile, width in stacked(result.shape[1]):
            here = (pl.ds(tile * CPG, CPG), pl.ds(0, width))
            value = result[step * CPAD : step * CPAD + CPG, tile * LANES : tile * LANES + width]
            sums[step][here] = value + partial[step][here] if partial else value
        if first:
            target = partner(own, step, grp)
            local = jnp.where(label[0:1] == target, label[1:2], -1)
            row = CPG * len(stacked(result.shape[1]))
            for kind in (local, spot, turn):
                for tile in range(lanes // LANES):
                    value = kind[:, tile * LANES : (tile + 1) * LANES].astype(F32)
                    sums[step][pl.ds(row, 1), :] = value
                    row += 1


def numerators(count, pieces, tags, arrived, chunk, edges, rows, steps, partial=()):
    mem, grp = lax.axis_size("mem"), lax.axis_size("grp")
    first = chunk == 0
    here = (rows[chunk], rows[chunk + 1])
    base = here[0] * ANGLES // LANES
    stop = min(-(-here[1] * ANGLES // LANES), edges[-1])
    segments, msgs = [], []
    for c in range(chunk + 1):
        low, high = max(edges[c], base), min(edges[c + 1], stop)
        if low < high:
            segments.append((c, edges[c + 1] - edges[c], low - edges[c], low - base, high - low))
            msgs += arrived[c] if c == 0 else arrived[c][slice(*steps)]
    lanes = (steps[1] - steps[0]) * CORES * count
    span = (here[1] - here[0]) * ANGLES
    tiles = stop - base
    shapes = [jax.ShapeDtypeStruct((ROWS, lanes), F32)] if first else []
    tall = sum_rows(span, lanes if first else 0)
    shapes += [jax.ShapeDtypeStruct((tall, LANES), F32)] * grp
    operands = [pieces] + ([] if first else [tags]) + msgs + list(partial)
    outs = pl.pallas_call(
        functools.partial(
            numer_kernel, mem, count, first, here, base, tiles, tuple(segments), steps, len(partial)
        ),
        out_shape=shapes,
        in_specs=[VMEM] * len(operands),
        out_specs=[VMEM] * len(shapes),
        scratch_shapes=[
            pltpu.VMEM((lanes, tiles * LANES), BF16),
            pltpu.VMEM((tiles * LANES, lanes), F32),
            pltpu.VMEM((span, 2 * lanes), BF16),
        ],
        name="numerators",
        **params(16),
    )(*operands)
    if first:
        return outs[0], outs[1:]
    return tags, outs


def denom_kernel(first, lanes, weights, *refs):
    blocks, (denom, spread) = refs[:-2], refs[-2:]
    span = weights.shape[0]
    klass = lax.broadcasted_iota(jnp.int32, (CPAD, lanes), 0)
    pair = lax.broadcasted_iota(jnp.int32, (PAIRS, lanes), 0)
    count = jnp.zeros((CPAD, PAIRS), F32)
    for ref in blocks:
        local, spot, turn = [label.astype(jnp.int32) for label in read_tags(ref, first, lanes)]
        member = (klass == local).astype(BF16)
        which = (pair == turn * BINS + spot).astype(BF16)
        count += lax.dot_general(member, which, NT, preferred_element_type=F32)
    high, low = split(count)
    left = jnp.concatenate(
        [jnp.concatenate([high, high], axis=1), jnp.concatenate([low, low], axis=1)], axis=0
    )

    def turn_far(q, carry):
        rows = pl.ds(pl.multiple_of(q * ANGLES, 2 * ROWS), ANGLES)
        block = weights[rows, :]
        for tile in range(PAIRS // LANES):
            far = turned(block, SHIFT * NEAR * tile)
            spread[rows, pl.ds(tile * LANES, LANES)] = far[:, :LANES]
            spread[rows, pl.ds(PAIRS + tile * LANES, LANES)] = far[:, LANES:]
        return carry

    lax.fori_loop(0, span // ANGLES, turn_far, 0, unroll=True)
    both = lax.dot_general(left, spread[...], NT, preferred_element_type=F32)
    denom[...] = both[:CPAD] + both[CPAD:]


def denominators(weights, blocks, first, lanes):
    span = weights.shape[0]
    return pl.pallas_call(
        functools.partial(denom_kernel, first, lanes),
        out_shape=jax.ShapeDtypeStruct((CPAD, span), F32),
        in_specs=[VMEM] * (1 + len(blocks)),
        out_specs=VMEM,
        scratch_shapes=[pltpu.VMEM((span, 2 * PAIRS), BF16)],
        name="denominators",
        **params(20),
    )(weights, *blocks)


def average_kernel(rows, denom, *refs):
    sums, out = refs[:-1], refs[-1]
    for chunk in range(len(rows) - 1):
        for tile, width in stacked((rows[chunk + 1] - rows[chunk]) * ANGLES):
            across = pl.ds(rows[chunk] * ANGLES + tile * LANES, width)
            total = sums[chunk][pl.ds(tile * CPG, CPG), pl.ds(0, width)]
            out[:, across] = total / (denom[:CPG, across] + wiener_term)


def averages(denom, sums, rows):
    span = denom.shape[1]
    return pl.pallas_call(
        functools.partial(average_kernel, rows),
        out_shape=jax.ShapeDtypeStruct((CPG, span), F32),
        in_specs=[VMEM] * (1 + len(sums)),
        out_specs=VMEM,
        name="averages",
        **params(8),
    )(denom, *sums)


def plan(span):
    turns = span // ANGLES
    tiles = -(-span // LANES)
    edges = [0, tiles // 2, tiles] if tiles % 2 == 0 else [0, tiles]
    rows = [min(edge * LANES // ANGLES, turns) for edge in edges]
    return tuple(edges), tuple(rows)


def on_device(images, classes, rotations, bins, ctf_table):
    mem, grp = lax.axis_size("mem"), lax.axis_size("grp")
    count = images.shape[0]
    span = images.shape[1] // mem
    edges, rows = plan(span)
    cols = edges[-1] * LANES
    places = mem // CORES
    table = ctf_table
    if cols != span:
        images = jnp.pad(images.reshape(count, mem, span), ((0, 0), (0, 0), (0, cols - span)))
        images = images.reshape(count, mem * cols)
        table = lax.dynamic_slice_in_dim(ctf_table, lax.axis_index("mem") * span, span, 1)
        table = jnp.pad(table, ((0, 0), (0, cols - span)))
    pieces, weights = tables(table, cols, span // ANGLES)
    firsts, seconds = pack(images, jnp.stack([classes, bins, rotations]), cols, edges)
    others = range(places - 1, 0, -1)
    here = {step: send(firsts[step], "mem", step, CORES) for step in others}
    here[0] = firsts[0]
    first = [here[step] for step in range(places)]
    arrived, after = [], [pieces]
    if seconds:
        kept, crossed = seconds[0], send(seconds[1], "mem", 0, CORES, 1)
        msgs = join(kept, crossed, [first[-1], pieces])
        here = {step: send(msgs[step], "mem", step, CORES) for step in others}
        here[0] = msgs[0]
        arrived, after = [[here[step] for step in range(places)]], [msgs[0]]
    arrived = [first + [send(cross(first, after), "mem", 0, CORES, 1)]] + arrived
    tags, sums, blocks = None, [], []
    for chunk in range(len(edges) - 1):
        cuts = [0, places]
        if chunk > 0 and places // 2 * CORES * count % LANES == 0:
            cuts = [0, places // 2, places]
        here = ()
        for steps in zip(cuts, cuts[1:]):
            tags, here = numerators(count, pieces, tags, arrived, chunk, edges, rows, steps, here)
        others = [send(here[step].astype(HALF), "grp", step) for step in range(1, grp)]
        if chunk == 0:
            blocks = [tag_block(part, rows[1] * ANGLES) for part in [here[0]] + others]
        total = here[0]
        for part in others:
            total = total + part.astype(F32)
        sums.append(total)
    denom = denominators(weights, blocks, rows[1] * ANGLES, mem * count)
    return averages(denom, sums, rows)


def solution(mesh):
    in_specs = (
        P(("grp", "mem"), None),
        P(("grp", "mem")),
        P(("grp", "mem")),
        P(("grp", "mem")),
        P(),
    )
    out_specs = P("grp", "mem")
    return jax.shard_map(
        on_device, mesh=mesh, in_specs=in_specs, out_specs=out_specs, check_vma=False
    )
```

```python
import functools

import jax
import jax.numpy as jnp
from jax import lax
from jax.experimental import pallas as pl
from jax.experimental.pallas import tpu as pltpu
from jax.sharding import PartitionSpec as P

ANGLES = 144
ROTS = 36
BINS = 16
CPG = 50
SHIFT = 4

LANES = 128
ROWS = 8
CORES = 2
CPAD = -(-CPG // ROWS) * ROWS
PIECES = 3
NEAR = LANES // BINS
PAIRS = -(-ROTS // NEAR) * LANES
LEVELS = max(ROTS - 1, 1).bit_length()

wiener_term = 1.0

F32 = jnp.float32
BF16 = jnp.bfloat16
HALF = jnp.float16
NT = (((1,), (1,)), ((), ()))
ANY = pl.BlockSpec(memory_space=pl.ANY)
HBM = pl.BlockSpec(memory_space=pltpu.HBM)
VMEM = pl.BlockSpec(memory_space=pltpu.VMEM)


def partner(index, step, size):
    if size & (size - 1) == 0:
        return index ^ step
    return lax.rem(index + step, size) if not isinstance(index, int) else (index + step) % size


def send(value, axis, step, cores=1, cross=0):
    size = lax.axis_size(axis) // cores
    pairs = [
        (i * cores + core, partner(i, step, size) * cores + (core ^ cross))
        for i in range(size)
        for core in range(cores)
    ]
    return lax.ppermute(value, axis, pairs)


def identity():
    rows = lax.broadcasted_iota(jnp.int32, (LANES, LANES), 0)
    cols = lax.broadcasted_iota(jnp.int32, (LANES, LANES), 1)
    return (rows == cols).astype(BF16)


def turned(block, amount):
    amount %= ANGLES
    if amount == 0:
        return block
    if amount % ROWS == 0:
        return jnp.concatenate([block[amount:], block[:amount]], axis=0)
    return pltpu.roll(block, ANGLES - amount, 0)


def split(value):
    high = value.astype(BF16)
    low = (value - high.astype(F32)).astype(BF16)
    return high, low


def params(mebibytes):
    return dict(
        compiler_params=pltpu.CompilerParams(vmem_limit_bytes=mebibytes << 20),
        cost_estimate=pl.CostEstimate(flops=1 << 20, bytes_accessed=1 << 16, transcendentals=0),
    )


def pack_kernel(mem, cols, edges, img, labels, *outs):
    places = mem // CORES
    count = img.shape[0]
    groups = count // ROWS
    here = lax.axis_index("mem") // CORES
    core = lax.rem(lax.axis_index("mem"), CORES)
    label = labels[0:1]
    owner = jnp.zeros_like(label)
    for g in range(1, lax.axis_size("grp")):
        owner += (label >= g * CPG).astype(jnp.int32)
    row = lax.broadcasted_iota(jnp.int32, (ROWS, count), 0) % (ROWS // CORES)
    stack = jnp.where(
        row == 0,
        owner,
        jnp.where(
            row == 1,
            label - owner * CPG,
            jnp.where(row == 2, labels[1:2], jnp.where(row == 3, labels[2:3], 0)),
        ),
    )
    spread = (
        lax.broadcasted_iota(jnp.int32, (count, LANES), 1) % count
        == lax.broadcasted_iota(jnp.int32, (count, LANES), 0)
    ).astype(BF16)
    tags = jnp.dot(stack.astype(F32).astype(BF16), spread, preferred_element_type=F32)
    place = lax.broadcasted_iota(jnp.int32, (ROWS, LANES), 1) // count
    lower = lax.broadcasted_iota(jnp.int32, (ROWS, LANES), 0) // (ROWS // CORES)
    for step in range(places):
        there = partner(here, step, places) * CORES
        slot = (step * CORES + lower) % (LANES // count)
        mine = jnp.where(place == slot, tags, 0.0).astype(BF16)
        for chunk in range(len(edges) - 1):
            width = (edges[chunk + 1] - edges[chunk]) * LANES
            for cross in range(CORES):
                out = outs[chunk * CORES + cross]
                start = (there + (core ^ cross)) * cols + edges[chunk] * LANES
                across = pl.ds(pl.multiple_of(start, LANES), width)
                for g in range(groups):
                    out[step, :, pl.ds(g * width, width)] = img[pl.ds(g * ROWS, ROWS), across]
                if chunk == 0:
                    out[step, :, pl.ds(groups * width, LANES)] = mine


def pack(images, labels, cols, edges):
    mem = lax.axis_size("mem")
    groups = images.shape[0] // ROWS
    shapes = []
    for chunk, (low, high) in enumerate(zip(edges, edges[1:])):
        width = groups * (high - low) * LANES + (0 if chunk else LANES)
        shapes += [jax.ShapeDtypeStruct((mem // CORES, ROWS, width), BF16)] * CORES
    outs = pl.pallas_call(
        functools.partial(pack_kernel, mem, cols, edges),
        out_shape=shapes,
        in_specs=[VMEM] * 2,
        out_specs=[VMEM] * len(shapes),
        name="pack",
        **params(8),
    )(images, labels)
    return list(zip(outs[::CORES], outs[1::CORES]))


def join_kernel(kept, crossed, *refs):
    places, _, span = kept.shape
    outs = refs[-places:]
    for step in range(places):
        outs[step][:, pl.ds(0, span)] = kept[step]
        outs[step][:, pl.ds(span, span)] = crossed[step]


def join(kept, crossed, after):
    places, _, span = kept.shape
    return pl.pallas_call(
        join_kernel,
        out_shape=[jax.ShapeDtypeStruct((ROWS, CORES * span), BF16)] * places,
        in_specs=[VMEM] * 2 + [ANY] * len(after),
        out_specs=[VMEM] * places,
        name="join",
        **params(8),
    )(kept, crossed, *after)


def table_kernel(turns, table, pieces, weights, ctf, square, sem):
    cols = ctf.shape[1]
    start = 0
    if table.shape[1] != cols:
        start = pl.multiple_of(lax.axis_index("mem") * cols, LANES)
    copy = pltpu.make_async_copy(table.at[:, pl.ds(start, cols)], ctf, sem)
    copy.start()
    copy.wait()
    value = ctf[...]
    high = value.astype(BF16).astype(F32)
    mid = (value - high).astype(BF16).astype(F32)
    low = value - high - mid
    stacked = jnp.concatenate([high, mid, low], axis=0).astype(BF16)
    eye = identity()
    pick = (
        lax.broadcasted_iota(jnp.int32, (PIECES * BINS, LANES), 0) % BINS
        == lax.broadcasted_iota(jnp.int32, (PIECES * BINS, LANES), 1) % BINS
    ).astype(BF16)
    for tile in range(cols // LANES):
        rows = pl.ds(tile * LANES, LANES)
        flipped = lax.dot_general(
            eye, stacked[:, tile * LANES : (tile + 1) * LANES], NT, preferred_element_type=F32
        ).astype(BF16)
        pieces[rows, :] = flipped
        spread = jnp.dot(flipped, pick, preferred_element_type=F32)
        square[rows, :] = spread * spread
    turn = lax.broadcasted_iota(jnp.int32, (1, LANES), 1) // BINS
    levels = max(NEAR - 1, 1).bit_length()

    def one(q, carry):
        rows = pl.ds(pl.multiple_of(q * ANGLES, 2 * ROWS), ANGLES)
        block = square[rows, :]
        for level in range(levels):
            chosen = (turn >> level & 1) == 1
            block = jnp.where(chosen, turned(block, SHIFT << level), block)
        high, low = split(block)
        weights[rows, pl.ds(0, LANES)] = high
        weights[rows, pl.ds(LANES, LANES)] = low
        return carry

    lax.fori_loop(0, turns, one, 0, unroll=2)


def tables(table, cols, turns):
    return pl.pallas_call(
        functools.partial(table_kernel, turns),
        out_shape=[
            jax.ShapeDtypeStruct((cols, PIECES * BINS), BF16),
            jax.ShapeDtypeStruct((turns * ANGLES, 2 * LANES), BF16),
        ],
        in_specs=[HBM],
        out_specs=[VMEM, VMEM],
        scratch_shapes=[
            pltpu.VMEM((BINS, cols), F32),
            pltpu.VMEM((cols, LANES), F32),
            pltpu.SemaphoreType.DMA,
        ],
        name="tables",
        **params(8),
    )(table)


def stacked(span):
    return [(low // LANES, min(LANES, span - low)) for low in range(0, span, LANES)]


def sum_rows(span, lanes):
    used = CPG * len(stacked(span)) + 3 * lanes // LANES
    return -(-used // ROWS) * ROWS


def tag_block(message, span):
    low = CPG * len(stacked(span)) // ROWS * ROWS
    return message[low:].astype(F32)


def read_tags(ref, span, lanes):
    rows = CPG * len(stacked(span))
    parts = lanes // LANES
    low = rows - rows // ROWS * ROWS
    return [
        jnp.concatenate([ref[pl.ds(low + kind * parts + part, 1), :] for part in range(parts)], axis=1)
        for kind in range(3)
    ]


def numer_kernel(mem, count, first, rows, base, tiles, segments, steps, added, ties, pieces, *refs):
    refs = list(refs)
    grp = lax.axis_size("grp")
    lanes = (steps[1] - steps[0]) * CORES * count
    groups = count // ROWS
    own = lax.axis_index("grp")
    if not first:
        tags = refs.pop(0)
    for chunk, wide, src, dst, width in segments:
        across = pl.ds(dst * LANES, width * LANES)
        taken = steps[1] - steps[0]
        msgs, refs = refs[:taken], refs[taken:]
        past = groups * wide * LANES
        far = past + (LANES if chunk == 0 else 0)
        for step in range(taken):
            for g in range(groups):
                low = (g * wide + src) * LANES
                at = step * CORES * count + g * ROWS
                for cross in range(CORES):
                    refs[-3][pl.ds(at + cross * count, ROWS), across] = msgs[step][
                        :, pl.ds(cross * far + low, width * LANES)
                    ]
    partial = refs[:added]
    refs = refs[added + ties :]
    if first:
        tags = refs.pop(0)
        per_tile = LANES // count
        half = ROWS // CORES
        for tile in range(lanes // LANES):
            total = jnp.zeros((ROWS, LANES), F32)
            for slot in range(tile * per_tile, (tile + 1) * per_tile, CORES):
                step = slot // CORES
                one = msgs[step][:, pl.ds(past, LANES)].astype(F32)
                other = msgs[step][:, pl.ds(far + past, LANES)].astype(F32)
                total += jnp.concatenate([one[:half] + other[half:], one[half:]], axis=0)
            tags[:, pl.ds(tile * LANES, LANES)] = total
    sums = refs[:grp]
    data, product, parts = refs[grp:]
    label = tags[:, pl.ds(steps[0] * CORES * count, lanes)].astype(jnp.int32)
    key = label[0:1] * CPAD + label[1:2]
    spot = label[2:3]
    turn = label[3:4]
    pick = (
        lax.broadcasted_iota(jnp.int32, (PIECES * BINS, lanes), 0) % BINS == spot
    ).astype(BF16)
    klass = lax.broadcasted_iota(jnp.int32, (CPAD, lanes), 0)
    member = []
    for step in range(grp):
        one = (klass + CPAD * partner(own, step, grp) == key).astype(BF16)
        member.append(jnp.concatenate([one, one], axis=1))
    eye = identity()
    for tile in range(tiles):
        across = pl.ds(tile * LANES, LANES)
        flipped = lax.dot_general(eye, data[:, across], NT, preferred_element_type=F32)
        ctf = jnp.dot(
            pieces[pl.ds((base + tile) * LANES, LANES), :], pick, preferred_element_type=F32
        )
        product[across, :] = flipped * ctf
    offset = rows[0] * ANGLES - base * LANES

    def rotate(q, carry):
        for tile in range(lanes // LANES):
            block = product[
                pl.ds(pl.multiple_of(offset + q * ANGLES, ROWS), ANGLES),
                pl.ds(tile * LANES, LANES),
            ]
            bits = turn[:, tile * LANES : (tile + 1) * LANES]
            for level in range(LEVELS):
                chosen = (bits >> level & 1) == 1
                block = jnp.where(chosen, turned(block, SHIFT << level), block)
            high, low = split(block)
            where = pl.ds(pl.multiple_of(q * ANGLES, 2 * ROWS), ANGLES)
            parts[where, pl.ds(tile * LANES, LANES)] = high
            parts[where, pl.ds(lanes + tile * LANES, LANES)] = low
        return carry

    lax.fori_loop(0, rows[1] - rows[0], rotate, 0, unroll=True)
    result = lax.dot_general(
        jnp.concatenate(member, axis=0), parts[...], NT, preferred_element_type=F32
    )
    for step in range(grp):
        for tile, width in stacked(result.shape[1]):
            here = (pl.ds(tile * CPG, CPG), pl.ds(0, width))
            value = result[step * CPAD : step * CPAD + CPG, tile * LANES : tile * LANES + width]
            sums[step][here] = value + partial[step][here] if partial else value
        if first:
            target = partner(own, step, grp)
            local = jnp.where(label[0:1] == target, label[1:2], -1)
            row = CPG * len(stacked(result.shape[1]))
            for kind in (local, spot, turn):
                for tile in range(lanes // LANES):
                    value = kind[:, tile * LANES : (tile + 1) * LANES].astype(F32)
                    sums[step][pl.ds(row, 1), :] = value
                    row += 1


def numerators(count, pieces, tags, arrived, chunk, edges, rows, steps, partial, after):
    mem, grp = lax.axis_size("mem"), lax.axis_size("grp")
    first = chunk == 0
    here = (rows[chunk], rows[chunk + 1])
    base = here[0] * ANGLES // LANES
    stop = min(-(-here[1] * ANGLES // LANES), edges[-1])
    segments, msgs = [], []
    for c in range(chunk + 1):
        low, high = max(edges[c], base), min(edges[c + 1], stop)
        if low < high:
            segments.append((c, edges[c + 1] - edges[c], low - edges[c], low - base, high - low))
            msgs += arrived[c][slice(*steps)]
    lanes = (steps[1] - steps[0]) * CORES * count
    span = (here[1] - here[0]) * ANGLES
    tiles = stop - base
    shapes = [jax.ShapeDtypeStruct((ROWS, lanes), F32)] if first else []
    tall = sum_rows(span, lanes if first else 0)
    shapes += [jax.ShapeDtypeStruct((tall, LANES), F32)] * grp
    operands = [pieces] + ([] if first else [tags]) + msgs + list(partial)
    outs = pl.pallas_call(
        functools.partial(
            numer_kernel, mem, count, first, here, base, tiles, tuple(segments), steps, len(partial),
            len(after),
        ),
        out_shape=shapes,
        in_specs=[VMEM] * len(operands) + [ANY] * len(after),
        out_specs=[VMEM] * len(shapes),
        scratch_shapes=[
            pltpu.VMEM((lanes, tiles * LANES), BF16),
            pltpu.VMEM((tiles * LANES, lanes), F32),
            pltpu.VMEM((span, 2 * lanes), BF16),
        ],
        name="numerators",
        **params(16),
    )(*operands, *after)
    if first:
        return outs[0], outs[1:]
    return tags, outs


def denom_kernel(first, lanes, weights, *refs):
    blocks, (denom, spread) = refs[:-2], refs[-2:]
    span = weights.shape[0]
    klass = lax.broadcasted_iota(jnp.int32, (CPAD, lanes), 0)
    pair = lax.broadcasted_iota(jnp.int32, (PAIRS, lanes), 0)
    count = jnp.zeros((CPAD, PAIRS), F32)
    for ref in blocks:
        local, spot, turn = [label.astype(jnp.int32) for label in read_tags(ref, first, lanes)]
        member = (klass == local).astype(BF16)
        which = (pair == turn * BINS + spot).astype(BF16)
        count += lax.dot_general(member, which, NT, preferred_element_type=F32)
    high, low = split(count)
    left = jnp.concatenate(
        [jnp.concatenate([high, high], axis=1), jnp.concatenate([low, low], axis=1)], axis=0
    )

    def turn_far(q, carry):
        rows = pl.ds(pl.multiple_of(q * ANGLES, 2 * ROWS), ANGLES)
        block = weights[rows, :]
        for tile in range(PAIRS // LANES):
            far = turned(block, SHIFT * NEAR * tile)
            spread[rows, pl.ds(tile * LANES, LANES)] = far[:, :LANES]
            spread[rows, pl.ds(PAIRS + tile * LANES, LANES)] = far[:, LANES:]
        return carry

    lax.fori_loop(0, span // ANGLES, turn_far, 0, unroll=True)
    both = lax.dot_general(left, spread[...], NT, preferred_element_type=F32)
    denom[...] = both[:CPAD] + both[CPAD:]


def denominators(weights, blocks, first, lanes):
    span = weights.shape[0]
    return pl.pallas_call(
        functools.partial(denom_kernel, first, lanes),
        out_shape=jax.ShapeDtypeStruct((CPAD, span), F32),
        in_specs=[VMEM] * (1 + len(blocks)),
        out_specs=VMEM,
        scratch_shapes=[pltpu.VMEM((span, 2 * PAIRS), BF16)],
        name="denominators",
        **params(20),
    )(weights, *blocks)


def average_kernel(rows, denom, *refs):
    sums, out = refs[:-1], refs[-1]
    for chunk in range(len(rows) - 1):
        for tile, width in stacked((rows[chunk + 1] - rows[chunk]) * ANGLES):
            across = pl.ds(rows[chunk] * ANGLES + tile * LANES, width)
            total = sums[chunk][pl.ds(tile * CPG, CPG), pl.ds(0, width)]
            out[:, across] = total / (denom[:CPG, across] + wiener_term)


def averages(denom, sums, rows):
    span = denom.shape[1]
    return pl.pallas_call(
        functools.partial(average_kernel, rows),
        out_shape=jax.ShapeDtypeStruct((CPG, span), F32),
        in_specs=[VMEM] * (1 + len(sums)),
        out_specs=VMEM,
        name="averages",
        **params(8),
    )(denom, *sums)


def plan(span):
    turns = span // ANGLES
    tiles = -(-span // LANES)
    edges = [0, tiles // 2, tiles] if tiles % 2 == 0 else [0, tiles]
    rows = [min(edge * LANES // ANGLES, turns) for edge in edges]
    return tuple(edges), tuple(rows)


def on_device(images, classes, rotations, bins, ctf_table):
    mem, grp = lax.axis_size("mem"), lax.axis_size("grp")
    count = images.shape[0]
    span = images.shape[1] // mem
    edges, rows = plan(span)
    cols = edges[-1] * LANES
    places = mem // CORES
    table = ctf_table
    if cols != span:
        images = jnp.pad(images.reshape(count, mem, span), ((0, 0), (0, 0), (0, cols - span)))
        images = images.reshape(count, mem * cols)
        table = lax.dynamic_slice_in_dim(ctf_table, lax.axis_index("mem") * span, span, 1)
        table = jnp.pad(table, ((0, 0), (0, cols - span)))
    pieces, weights = tables(table, cols, span // ANGLES)
    chunks = pack(images, jnp.stack([classes, bins, rotations]), cols, edges)
    arrived, after, ties = [], [], []
    for kept, crossed in chunks:
        msgs = join(kept, send(crossed, "mem", 0, CORES, 1), after)
        here = {step: send(msgs[step], "mem", step, CORES) for step in range(places - 1, 0, -1)}
        here[0] = msgs[0]
        arrived.append([here[step] for step in range(places)])
        after = [pieces]
        ties = [msgs[0]] if len(arrived) > 1 else []
    tags, sums, blocks = None, [], []
    for chunk in range(len(edges) - 1):
        cuts = [0, places]
        if chunk > 0 and places // 2 * CORES * count % LANES == 0:
            cuts = [0, places // 2, places]
        here = ()
        for steps in zip(cuts, cuts[1:]):
            tie = [] if chunk else ties
            tags, here = numerators(
                count, pieces, tags, arrived, chunk, edges, rows, steps, here, tie
            )
        others = [send(here[step].astype(HALF), "grp", step) for step in range(1, grp)]
        if chunk == 0:
            blocks = [tag_block(part, rows[1] * ANGLES) for part in [here[0]] + others]
        total = here[0]
        for part in others:
            total = total + part.astype(F32)
        sums.append(total)
    denom = denominators(weights, blocks, rows[1] * ANGLES, mem * count)
    return averages(denom, sums, rows)


def solution(mesh):
    in_specs = (
        P(("grp", "mem"), None),
        P(("grp", "mem")),
        P(("grp", "mem")),
        P(("grp", "mem")),
        P(),
    )
    out_specs = P("grp", "mem")
    return jax.shard_map(
        on_device, mesh=mesh, in_specs=in_specs, out_specs=out_specs, check_vma=False
    )
```

```python
import functools

import jax
import jax.numpy as jnp
from jax import lax
from jax.experimental import pallas as pl
from jax.experimental.pallas import tpu as pltpu
from jax.sharding import PartitionSpec as P

ANGLES = 144
ROTS = 36
BINS = 16
CPG = 50
SHIFT = 4

LANES = 128
ROWS = 8
CORES = 2
CPAD = -(-CPG // ROWS) * ROWS
PIECES = 3
NEAR = LANES // BINS
PAIRS = -(-ROTS // NEAR) * LANES
LEVELS = max(ROTS - 1, 1).bit_length()

wiener_term = 1.0

F32 = jnp.float32
BF16 = jnp.bfloat16
HALF = jnp.float16
NT = (((1,), (1,)), ((), ()))
ANY = pl.BlockSpec(memory_space=pl.ANY)
HBM = pl.BlockSpec(memory_space=pltpu.HBM)
VMEM = pl.BlockSpec(memory_space=pltpu.VMEM)


def partner(index, step, size):
    if size & (size - 1) == 0:
        return index ^ step
    return lax.rem(index + step, size) if not isinstance(index, int) else (index + step) % size


def send(value, axis, step, cores=1, cross=0):
    size = lax.axis_size(axis) // cores
    pairs = [
        (i * cores + core, partner(i, step, size) * cores + (core ^ cross))
        for i in range(size)
        for core in range(cores)
    ]
    return lax.ppermute(value, axis, pairs)


def identity():
    rows = lax.broadcasted_iota(jnp.int32, (LANES, LANES), 0)
    cols = lax.broadcasted_iota(jnp.int32, (LANES, LANES), 1)
    return (rows == cols).astype(BF16)


def turned(block, amount):
    amount %= ANGLES
    if amount == 0:
        return block
    if amount % ROWS == 0:
        return jnp.concatenate([block[amount:], block[:amount]], axis=0)
    return pltpu.roll(block, ANGLES - amount, 0)


def split(value):
    high = value.astype(BF16)
    low = (value - high.astype(F32)).astype(BF16)
    return high, low


def params(mebibytes):
    return dict(
        compiler_params=pltpu.CompilerParams(vmem_limit_bytes=mebibytes << 20),
        cost_estimate=pl.CostEstimate(flops=1 << 20, bytes_accessed=1 << 16, transcendentals=0),
    )


def pack_kernel(mem, cols, edges, img, labels, *outs):
    places = mem // CORES
    count = img.shape[0]
    groups = count // ROWS
    here = lax.axis_index("mem") // CORES
    core = lax.rem(lax.axis_index("mem"), CORES)
    label = labels[0:1]
    owner = jnp.zeros_like(label)
    for g in range(1, lax.axis_size("grp")):
        owner += (label >= g * CPG).astype(jnp.int32)
    row = lax.broadcasted_iota(jnp.int32, (ROWS, count), 0) % (ROWS // CORES)
    stack = jnp.where(
        row == 0,
        owner,
        jnp.where(
            row == 1,
            label - owner * CPG,
            jnp.where(row == 2, labels[1:2], jnp.where(row == 3, labels[2:3], 0)),
        ),
    )
    spread = (
        lax.broadcasted_iota(jnp.int32, (count, LANES), 1) % count
        == lax.broadcasted_iota(jnp.int32, (count, LANES), 0)
    ).astype(BF16)
    tags = jnp.dot(stack.astype(F32).astype(BF16), spread, preferred_element_type=F32)
    place = lax.broadcasted_iota(jnp.int32, (ROWS, LANES), 1) // count
    lower = lax.broadcasted_iota(jnp.int32, (ROWS, LANES), 0) // (ROWS // CORES)
    for step in range(places):
        there = partner(here, step, places) * CORES
        slot = (step * CORES + lower) % (LANES // count)
        mine = jnp.where(place == slot, tags, 0.0).astype(BF16)
        for chunk in range(len(edges) - 1):
            width = (edges[chunk + 1] - edges[chunk]) * LANES
            for cross in range(CORES):
                out = outs[chunk * CORES + cross]
                start = (there + (core ^ cross)) * cols + edges[chunk] * LANES
                across = pl.ds(pl.multiple_of(start, LANES), width)
                for g in range(groups):
                    out[step, :, pl.ds(g * width, width)] = img[pl.ds(g * ROWS, ROWS), across]
                if chunk == 0:
                    out[step, :, pl.ds(groups * width, LANES)] = mine


def pack(images, labels, cols, edges):
    mem = lax.axis_size("mem")
    groups = images.shape[0] // ROWS
    shapes = []
    for chunk, (low, high) in enumerate(zip(edges, edges[1:])):
        width = groups * (high - low) * LANES + (0 if chunk else LANES)
        shapes += [jax.ShapeDtypeStruct((mem // CORES, ROWS, width), BF16)] * CORES
    outs = pl.pallas_call(
        functools.partial(pack_kernel, mem, cols, edges),
        out_shape=shapes,
        in_specs=[VMEM] * 2,
        out_specs=[VMEM] * len(shapes),
        name="pack",
        **params(8),
    )(images, labels)
    return list(zip(outs[::CORES], outs[1::CORES]))


def join_kernel(kept, crossed, *refs):
    places, _, span = kept.shape
    outs = refs[-places:]
    for step in range(places):
        outs[step][:, pl.ds(0, span)] = kept[step]
        outs[step][:, pl.ds(span, span)] = crossed[step]


def join(kept, crossed, after):
    places, _, span = kept.shape
    return pl.pallas_call(
        join_kernel,
        out_shape=[jax.ShapeDtypeStruct((ROWS, CORES * span), BF16)] * places,
        in_specs=[VMEM] * 2 + [ANY] * len(after),
        out_specs=[VMEM] * places,
        name="join",
        **params(8),
    )(kept, crossed, *after)


def table_kernel(turns, table, pieces, weights, ctf, square, sem):
    cols = ctf.shape[1]
    start = 0
    if table.shape[1] != cols:
        start = pl.multiple_of(lax.axis_index("mem") * cols, LANES)
    copy = pltpu.make_async_copy(table.at[:, pl.ds(start, cols)], ctf, sem)
    copy.start()
    copy.wait()
    value = ctf[...]
    high = value.astype(BF16).astype(F32)
    mid = (value - high).astype(BF16).astype(F32)
    low = value - high - mid
    stacked = jnp.concatenate([high, mid, low], axis=0).astype(BF16)
    eye = identity()
    pick = (
        lax.broadcasted_iota(jnp.int32, (PIECES * BINS, LANES), 0) % BINS
        == lax.broadcasted_iota(jnp.int32, (PIECES * BINS, LANES), 1) % BINS
    ).astype(BF16)
    for tile in range(cols // LANES):
        rows = pl.ds(tile * LANES, LANES)
        flipped = lax.dot_general(
            eye, stacked[:, tile * LANES : (tile + 1) * LANES], NT, preferred_element_type=F32
        ).astype(BF16)
        pieces[rows, :] = flipped
        spread = jnp.dot(flipped, pick, preferred_element_type=F32)
        square[rows, :] = spread * spread
    turn = lax.broadcasted_iota(jnp.int32, (1, LANES), 1) // BINS
    levels = max(NEAR - 1, 1).bit_length()

    def one(q, carry):
        rows = pl.ds(pl.multiple_of(q * ANGLES, 2 * ROWS), ANGLES)
        block = square[rows, :]
        for level in range(levels):
            chosen = (turn >> level & 1) == 1
            block = jnp.where(chosen, turned(block, SHIFT << level), block)
        high, low = split(block)
        weights[rows, pl.ds(0, LANES)] = high
        weights[rows, pl.ds(LANES, LANES)] = low
        return carry

    lax.fori_loop(0, turns, one, 0, unroll=2)


def tables(table, cols, turns):
    return pl.pallas_call(
        functools.partial(table_kernel, turns),
        out_shape=[
            jax.ShapeDtypeStruct((cols, PIECES * BINS), BF16),
            jax.ShapeDtypeStruct((turns * ANGLES, 2 * LANES), BF16),
        ],
        in_specs=[HBM],
        out_specs=[VMEM, VMEM],
        scratch_shapes=[
            pltpu.VMEM((BINS, cols), F32),
            pltpu.VMEM((cols, LANES), F32),
            pltpu.SemaphoreType.DMA,
        ],
        name="tables",
        **params(8),
    )(table)


def stacked(span):
    return [(low // LANES, min(LANES, span - low)) for low in range(0, span, LANES)]


def sum_rows(span, lanes):
    used = CPG * len(stacked(span)) + 3 * lanes // LANES
    return -(-used // ROWS) * ROWS


def tag_block(message, span):
    low = CPG * len(stacked(span)) // ROWS * ROWS
    return message[low:].astype(F32)


def read_tags(ref, span, lanes):
    rows = CPG * len(stacked(span))
    parts = lanes // LANES
    low = rows - rows // ROWS * ROWS
    return [
        jnp.concatenate([ref[pl.ds(low + kind * parts + part, 1), :] for part in range(parts)], axis=1)
        for kind in range(3)
    ]


def numer_kernel(mem, count, first, rows, base, tiles, segments, steps, added, ties, pieces, *refs):
    refs = list(refs)
    grp = lax.axis_size("grp")
    lanes = (steps[1] - steps[0]) * CORES * count
    groups = count // ROWS
    own = lax.axis_index("grp")
    if not first:
        tags = refs.pop(0)
    elif added:
        earlier = refs.pop(0)
    for chunk, wide, src, dst, width in segments:
        across = pl.ds(dst * LANES, width * LANES)
        taken = steps[1] - steps[0]
        msgs, refs = refs[:taken], refs[taken:]
        past = groups * wide * LANES
        far = past + (LANES if chunk == 0 else 0)
        for step in range(taken):
            for g in range(groups):
                low = (g * wide + src) * LANES
                at = step * CORES * count + g * ROWS
                for cross in range(CORES):
                    refs[-3][pl.ds(at + cross * count, ROWS), across] = msgs[step][
                        :, pl.ds(cross * far + low, width * LANES)
                    ]
    partial = refs[:added]
    refs = refs[added + ties :]
    if first:
        tags = refs.pop(0)
        per_tile = LANES // count
        half = ROWS // CORES
        for tile in range(lanes // LANES):
            total = jnp.zeros((ROWS, LANES), F32)
            for slot in range(tile * per_tile, (tile + 1) * per_tile, CORES):
                step = slot // CORES
                one = msgs[step][:, pl.ds(past, LANES)].astype(F32)
                other = msgs[step][:, pl.ds(far + past, LANES)].astype(F32)
                total += jnp.concatenate([one[:half] + other[half:], one[half:]], axis=0)
            tags[:, pl.ds(tile * LANES, LANES)] = total
    sums = refs[:grp]
    data, product, parts = refs[grp:]
    label = tags[...].astype(jnp.int32)
    key = label[0:1] * CPAD + label[1:2]
    spot = label[2:3]
    turn = label[3:4]
    pick = (
        lax.broadcasted_iota(jnp.int32, (PIECES * BINS, lanes), 0) % BINS == spot
    ).astype(BF16)
    klass = lax.broadcasted_iota(jnp.int32, (CPAD, lanes), 0)
    member = []
    for step in range(grp):
        one = (klass + CPAD * partner(own, step, grp) == key).astype(BF16)
        member.append(jnp.concatenate([one, one], axis=1))
    eye = identity()
    for tile in range(tiles):
        across = pl.ds(tile * LANES, LANES)
        flipped = lax.dot_general(eye, data[:, across], NT, preferred_element_type=F32)
        ctf = jnp.dot(
            pieces[pl.ds((base + tile) * LANES, LANES), :], pick, preferred_element_type=F32
        )
        product[across, :] = flipped * ctf
    offset = rows[0] * ANGLES - base * LANES

    def rotate(q, carry):
        for tile in range(lanes // LANES):
            block = product[
                pl.ds(pl.multiple_of(offset + q * ANGLES, ROWS), ANGLES),
                pl.ds(tile * LANES, LANES),
            ]
            bits = turn[:, tile * LANES : (tile + 1) * LANES]
            for level in range(LEVELS):
                chosen = (bits >> level & 1) == 1
                block = jnp.where(chosen, turned(block, SHIFT << level), block)
            high, low = split(block)
            where = pl.ds(pl.multiple_of(q * ANGLES, 2 * ROWS), ANGLES)
            parts[where, pl.ds(tile * LANES, LANES)] = high
            parts[where, pl.ds(lanes + tile * LANES, LANES)] = low
        return carry

    lax.fori_loop(0, rows[1] - rows[0], rotate, 0, unroll=True)
    result = lax.dot_general(
        jnp.concatenate(member, axis=0), parts[...], NT, preferred_element_type=F32
    )
    for step in range(grp):
        for tile, width in stacked(result.shape[1]):
            here = (pl.ds(tile * CPG, CPG), pl.ds(0, width))
            value = result[step * CPAD : step * CPAD + CPG, tile * LANES : tile * LANES + width]
            sums[step][here] = value + partial[step][here] if partial else value
        if first and steps[1] == mem // CORES:
            every = label
            if added:
                every = jnp.concatenate([earlier[...].astype(jnp.int32), label], axis=1)
            target = partner(own, step, grp)
            local = jnp.where(every[0:1] == target, every[1:2], -1)
            row = CPG * len(stacked(result.shape[1]))
            for kind in (local, every[2:3], every[3:4]):
                for tile in range(every.shape[1] // LANES):
                    value = kind[:, tile * LANES : (tile + 1) * LANES].astype(F32)
                    sums[step][pl.ds(row, 1), :] = value
                    row += 1


def numerators(count, pieces, tags, arrived, chunk, edges, rows, steps, partial, after):
    mem, grp = lax.axis_size("mem"), lax.axis_size("grp")
    first = chunk == 0
    here = (rows[chunk], rows[chunk + 1])
    base = here[0] * ANGLES // LANES
    stop = min(-(-here[1] * ANGLES // LANES), edges[-1])
    segments, msgs = [], []
    for c in range(chunk + 1):
        low, high = max(edges[c], base), min(edges[c + 1], stop)
        if low < high:
            segments.append((c, edges[c + 1] - edges[c], low - edges[c], low - base, high - low))
            msgs += arrived[c][slice(*steps)]
    lanes = (steps[1] - steps[0]) * CORES * count
    span = (here[1] - here[0]) * ANGLES
    tiles = stop - base
    shapes = [jax.ShapeDtypeStruct((ROWS, lanes), F32)] if first else []
    tall = sum_rows(span, mem * count if first else 0)
    shapes += [jax.ShapeDtypeStruct((tall, LANES), F32)] * grp
    operands = [pieces] + ([] if tags is None else [tags]) + msgs + list(partial)
    outs = pl.pallas_call(
        functools.partial(
            numer_kernel, mem, count, first, here, base, tiles, tuple(segments), steps, len(partial),
            len(after),
        ),
        out_shape=shapes,
        in_specs=[VMEM] * len(operands) + [ANY] * len(after),
        out_specs=[VMEM] * len(shapes),
        scratch_shapes=[
            pltpu.VMEM((lanes, tiles * LANES), BF16),
            pltpu.VMEM((tiles * LANES, lanes), F32),
            pltpu.VMEM((span, 2 * lanes), BF16),
        ],
        name="numerators",
        **params(16),
    )(*operands, *after)
    if first:
        return outs[0], outs[1:]
    return tags, outs


def denom_kernel(first, lanes, weights, *refs):
    blocks, (denom, spread) = refs[:-2], refs[-2:]
    span = weights.shape[0]
    klass = lax.broadcasted_iota(jnp.int32, (CPAD, lanes), 0)
    pair = lax.broadcasted_iota(jnp.int32, (PAIRS, lanes), 0)
    count = jnp.zeros((CPAD, PAIRS), F32)
    for ref in blocks:
        local, spot, turn = [label.astype(jnp.int32) for label in read_tags(ref, first, lanes)]
        member = (klass == local).astype(BF16)
        which = (pair == turn * BINS + spot).astype(BF16)
        count += lax.dot_general(member, which, NT, preferred_element_type=F32)
    high, low = split(count)
    left = jnp.concatenate(
        [jnp.concatenate([high, high], axis=1), jnp.concatenate([low, low], axis=1)], axis=0
    )

    def turn_far(q, carry):
        rows = pl.ds(pl.multiple_of(q * ANGLES, 2 * ROWS), ANGLES)
        block = weights[rows, :]
        for tile in range(PAIRS // LANES):
            far = turned(block, SHIFT * NEAR * tile)
            spread[rows, pl.ds(tile * LANES, LANES)] = far[:, :LANES]
            spread[rows, pl.ds(PAIRS + tile * LANES, LANES)] = far[:, LANES:]
        return carry

    lax.fori_loop(0, span // ANGLES, turn_far, 0, unroll=True)
    both = lax.dot_general(left, spread[...], NT, preferred_element_type=F32)
    denom[...] = both[:CPAD] + both[CPAD:]


def denominators(weights, blocks, first, lanes):
    span = weights.shape[0]
    return pl.pallas_call(
        functools.partial(denom_kernel, first, lanes),
        out_shape=jax.ShapeDtypeStruct((CPAD, span), F32),
        in_specs=[VMEM] * (1 + len(blocks)),
        out_specs=VMEM,
        scratch_shapes=[pltpu.VMEM((span, 2 * PAIRS), BF16)],
        name="denominators",
        **params(20),
    )(weights, *blocks)


def average_kernel(rows, denom, *refs):
    sums, out = refs[:-1], refs[-1]
    for chunk in range(len(rows) - 1):
        for tile, width in stacked((rows[chunk + 1] - rows[chunk]) * ANGLES):
            across = pl.ds(rows[chunk] * ANGLES + tile * LANES, width)
            total = sums[chunk][pl.ds(tile * CPG, CPG), pl.ds(0, width)]
            out[:, across] = total / (denom[:CPG, across] + wiener_term)


def averages(denom, sums, rows):
    span = denom.shape[1]
    return pl.pallas_call(
        functools.partial(average_kernel, rows),
        out_shape=jax.ShapeDtypeStruct((CPG, span), F32),
        in_specs=[VMEM] * (1 + len(sums)),
        out_specs=VMEM,
        name="averages",
        **params(8),
    )(denom, *sums)


def plan(span):
    turns = span // ANGLES
    tiles = -(-span // LANES)
    edges = [0, tiles // 2, tiles] if tiles % 2 == 0 else [0, tiles]
    rows = [min(edge * LANES // ANGLES, turns) for edge in edges]
    return tuple(edges), tuple(rows)


def on_device(images, classes, rotations, bins, ctf_table):
    mem, grp = lax.axis_size("mem"), lax.axis_size("grp")
    count = images.shape[0]
    span = images.shape[1] // mem
    edges, rows = plan(span)
    cols = edges[-1] * LANES
    places = mem // CORES
    table = ctf_table
    if cols != span:
        images = jnp.pad(images.reshape(count, mem, span), ((0, 0), (0, 0), (0, cols - span)))
        images = images.reshape(count, mem * cols)
        table = lax.dynamic_slice_in_dim(ctf_table, lax.axis_index("mem") * span, span, 1)
        table = jnp.pad(table, ((0, 0), (0, cols - span)))
    pieces, weights = tables(table, cols, span // ANGLES)
    chunks = pack(images, jnp.stack([classes, bins, rotations]), cols, edges)
    arrived, after, ties = [], [], []
    for kept, crossed in chunks:
        msgs = join(kept, send(crossed, "mem", 0, CORES, 1), after)
        here = {step: send(msgs[step], "mem", step, CORES) for step in range(places - 1, 0, -1)}
        here[0] = msgs[0]
        arrived.append([here[step] for step in range(places)])
        after = [pieces]
        ties = [msgs[0]] if len(arrived) > 1 else []
    tags, sums, blocks = [], [], []
    for chunk in range(len(edges) - 1):
        cuts = [0, places]
        if places // 2 * CORES * count % LANES == 0:
            cuts = [0, places // 2, places]
        here, last = (), None
        for part, steps in enumerate(zip(cuts, cuts[1:])):
            known, tie = (tags[part], []) if chunk else (last, ties)
            last, here = numerators(
                count, pieces, known, arrived, chunk, edges, rows, steps, here, tie
            )
            if chunk == 0:
                tags.append(last)
        others = [send(here[step].astype(HALF), "grp", step) for step in range(1, grp)]
        if chunk == 0:
            blocks = [tag_block(part, rows[1] * ANGLES) for part in [here[0]] + others]
        total = here[0]
        for part in others:
            total = total + part.astype(F32)
        sums.append(total)
    denom = denominators(weights, blocks, rows[1] * ANGLES, mem * count)
    return averages(denom, sums, rows)


def solution(mesh):
    in_specs = (
        P(("grp", "mem"), None),
        P(("grp", "mem")),
        P(("grp", "mem")),
        P(("grp", "mem")),
        P(),
    )
    out_specs = P("grp", "mem")
    return jax.shard_map(
        on_device, mesh=mesh, in_specs=in_specs, out_specs=out_specs, check_vma=False
    )
```

```python
import functools

import jax
import jax.numpy as jnp
from jax import lax
from jax.experimental import pallas as pl
from jax.experimental.pallas import tpu as pltpu
from jax.sharding import PartitionSpec as P

ANGLES = 144
ROTS = 36
BINS = 16
CPG = 50
SHIFT = 4

LANES = 128
ROWS = 8
CORES = 2
CPAD = -(-CPG // ROWS) * ROWS
PIECES = 3
NEAR = LANES // BINS
PAIRS = -(-ROTS // NEAR) * LANES
LEVELS = max(ROTS - 1, 1).bit_length()

wiener_term = 1.0

F32 = jnp.float32
BF16 = jnp.bfloat16
HALF = jnp.float16
NT = (((1,), (1,)), ((), ()))
ANY = pl.BlockSpec(memory_space=pl.ANY)
HBM = pl.BlockSpec(memory_space=pltpu.HBM)
VMEM = pl.BlockSpec(memory_space=pltpu.VMEM)


def partner(index, step, size):
    if size & (size - 1) == 0:
        return index ^ step
    return lax.rem(index + step, size) if not isinstance(index, int) else (index + step) % size


def send(value, axis, step, cores=1, cross=0):
    size = lax.axis_size(axis) // cores
    pairs = [
        (i * cores + core, partner(i, step, size) * cores + (core ^ cross))
        for i in range(size)
        for core in range(cores)
    ]
    return lax.ppermute(value, axis, pairs)


def identity():
    rows = lax.broadcasted_iota(jnp.int32, (LANES, LANES), 0)
    cols = lax.broadcasted_iota(jnp.int32, (LANES, LANES), 1)
    return (rows == cols).astype(BF16)


def turned(block, amount):
    amount %= ANGLES
    if amount == 0:
        return block
    if amount % ROWS == 0:
        return jnp.concatenate([block[amount:], block[:amount]], axis=0)
    return pltpu.roll(block, ANGLES - amount, 0)


def split(value):
    high = value.astype(BF16)
    low = (value - high.astype(F32)).astype(BF16)
    return high, low


def params(mebibytes):
    return dict(
        compiler_params=pltpu.CompilerParams(vmem_limit_bytes=mebibytes << 20),
        cost_estimate=pl.CostEstimate(flops=1 << 20, bytes_accessed=1 << 16, transcendentals=0),
    )


def pack_kernel(mem, cols, edges, img, labels, *outs):
    places = mem // CORES
    count = img.shape[0]
    groups = count // ROWS
    here = lax.axis_index("mem") // CORES
    core = lax.rem(lax.axis_index("mem"), CORES)
    label = labels[0:1]
    owner = jnp.zeros_like(label)
    for g in range(1, lax.axis_size("grp")):
        owner += (label >= g * CPG).astype(jnp.int32)
    row = lax.broadcasted_iota(jnp.int32, (ROWS, count), 0) % (ROWS // CORES)
    stack = jnp.where(
        row == 0,
        owner,
        jnp.where(
            row == 1,
            label - owner * CPG,
            jnp.where(row == 2, labels[1:2], jnp.where(row == 3, labels[2:3], 0)),
        ),
    )
    spread = (
        lax.broadcasted_iota(jnp.int32, (count, LANES), 1) % count
        == lax.broadcasted_iota(jnp.int32, (count, LANES), 0)
    ).astype(BF16)
    tags = jnp.dot(stack.astype(F32).astype(BF16), spread, preferred_element_type=F32)
    place = lax.broadcasted_iota(jnp.int32, (ROWS, LANES), 1) // count
    lower = lax.broadcasted_iota(jnp.int32, (ROWS, LANES), 0) // (ROWS // CORES)
    for step in range(places):
        there = partner(here, step, places) * CORES
        slot = (step * CORES + lower) % (LANES // count)
        mine = jnp.where(place == slot, tags, 0.0).astype(BF16)
        for chunk in range(len(edges) - 1):
            width = (edges[chunk + 1] - edges[chunk]) * LANES
            for cross in range(CORES):
                out = outs[chunk * CORES + cross]
                start = (there + (core ^ cross)) * cols + edges[chunk] * LANES
                across = pl.ds(pl.multiple_of(start, LANES), width)
                for g in range(groups):
                    out[step, :, pl.ds(g * width, width)] = img[pl.ds(g * ROWS, ROWS), across]
                if chunk == 0:
                    out[step, :, pl.ds(groups * width, LANES)] = mine


def pack(images, labels, cols, edges):
    mem = lax.axis_size("mem")
    groups = images.shape[0] // ROWS
    shapes = []
    for chunk, (low, high) in enumerate(zip(edges, edges[1:])):
        width = groups * (high - low) * LANES + (0 if chunk else LANES)
        shapes += [jax.ShapeDtypeStruct((mem // CORES, ROWS, width), BF16)] * CORES
    outs = pl.pallas_call(
        functools.partial(pack_kernel, mem, cols, edges),
        out_shape=shapes,
        in_specs=[VMEM] * 2,
        out_specs=[VMEM] * len(shapes),
        name="pack",
        **params(8),
    )(images, labels)
    return list(zip(outs[::CORES], outs[1::CORES]))


def join_kernel(kept, crossed, *refs):
    places, _, span = kept.shape
    outs = refs[-places:]
    for step in range(places):
        outs[step][:, pl.ds(0, span)] = kept[step]
        outs[step][:, pl.ds(span, span)] = crossed[step]


def join(kept, crossed, after):
    places, _, span = kept.shape
    return pl.pallas_call(
        join_kernel,
        out_shape=[jax.ShapeDtypeStruct((ROWS, CORES * span), BF16)] * places,
        in_specs=[VMEM] * 2 + [ANY] * len(after),
        out_specs=[VMEM] * places,
        name="join",
        **params(8),
    )(kept, crossed, *after)


def table_kernel(turns, table, pieces, weights, ctf, square, sem):
    cols = ctf.shape[1]
    start = 0
    if table.shape[1] != cols:
        start = pl.multiple_of(lax.axis_index("mem") * cols, LANES)
    copy = pltpu.make_async_copy(table.at[:, pl.ds(start, cols)], ctf, sem)
    copy.start()
    copy.wait()
    value = ctf[...]
    high = value.astype(BF16).astype(F32)
    mid = (value - high).astype(BF16).astype(F32)
    low = value - high - mid
    stacked = jnp.concatenate([high, mid, low], axis=0).astype(BF16)
    eye = identity()
    pick = (
        lax.broadcasted_iota(jnp.int32, (PIECES * BINS, LANES), 0) % BINS
        == lax.broadcasted_iota(jnp.int32, (PIECES * BINS, LANES), 1) % BINS
    ).astype(BF16)
    for tile in range(cols // LANES):
        rows = pl.ds(tile * LANES, LANES)
        flipped = lax.dot_general(
            eye, stacked[:, tile * LANES : (tile + 1) * LANES], NT, preferred_element_type=F32
        ).astype(BF16)
        pieces[rows, :] = flipped
        spread = jnp.dot(flipped, pick, preferred_element_type=F32)
        square[rows, :] = spread * spread
    turn = lax.broadcasted_iota(jnp.int32, (1, LANES), 1) // BINS
    levels = max(NEAR - 1, 1).bit_length()

    def one(q, carry):
        rows = pl.ds(pl.multiple_of(q * ANGLES, 2 * ROWS), ANGLES)
        block = square[rows, :]
        for level in range(levels):
            chosen = (turn >> level & 1) == 1
            block = jnp.where(chosen, turned(block, SHIFT << level), block)
        high, low = split(block)
        weights[rows, pl.ds(0, LANES)] = high
        weights[rows, pl.ds(LANES, LANES)] = low
        return carry

    lax.fori_loop(0, turns, one, 0, unroll=2)


def tables(table, cols, turns):
    return pl.pallas_call(
        functools.partial(table_kernel, turns),
        out_shape=[
            jax.ShapeDtypeStruct((cols, PIECES * BINS), BF16),
            jax.ShapeDtypeStruct((turns * ANGLES, 2 * LANES), BF16),
        ],
        in_specs=[HBM],
        out_specs=[VMEM, VMEM],
        scratch_shapes=[
            pltpu.VMEM((BINS, cols), F32),
            pltpu.VMEM((cols, LANES), F32),
            pltpu.SemaphoreType.DMA,
        ],
        name="tables",
        **params(8),
    )(table)


def stacked(span):
    return [(low // LANES, min(LANES, span - low)) for low in range(0, span, LANES)]


def sum_rows(span, lanes):
    used = CPG * len(stacked(span)) + 3 * lanes // LANES
    return -(-used // ROWS) * ROWS


def tag_block(message, span):
    low = CPG * len(stacked(span)) // ROWS * ROWS
    return message[low:].astype(F32)


def read_tags(ref, span, lanes):
    rows = CPG * len(stacked(span))
    parts = lanes // LANES
    low = rows - rows // ROWS * ROWS
    return [
        jnp.concatenate([ref[pl.ds(low + kind * parts + part, 1), :] for part in range(parts)], axis=1)
        for kind in range(3)
    ]


def numer_kernel(mem, count, first, rows, base, tiles, segments, steps, added, ties, pieces, *refs):
    refs = list(refs)
    grp = lax.axis_size("grp")
    lanes = (steps[1] - steps[0]) * CORES * count
    groups = count // ROWS
    own = lax.axis_index("grp")
    if not first:
        tags = refs.pop(0)
    for chunk, wide, src, dst, width in segments:
        across = pl.ds(dst * LANES, width * LANES)
        taken = steps[1] - steps[0]
        msgs, refs = refs[:taken], refs[taken:]
        past = groups * wide * LANES
        far = past + (LANES if chunk == 0 else 0)
        for step in range(taken):
            for g in range(groups):
                low = (g * wide + src) * LANES
                at = step * CORES * count + g * ROWS
                for cross in range(CORES):
                    refs[-3][pl.ds(at + cross * count, ROWS), across] = msgs[step][
                        :, pl.ds(cross * far + low, width * LANES)
                    ]
    partial = refs[:added]
    refs = refs[added + ties :]
    if first:
        tags = refs.pop(0)
        per_tile = LANES // count
        half = ROWS // CORES
        for tile in range(lanes // LANES):
            total = jnp.zeros((ROWS, LANES), F32)
            for slot in range(tile * per_tile, (tile + 1) * per_tile, CORES):
                step = slot // CORES
                one = msgs[step][:, pl.ds(past, LANES)].astype(F32)
                other = msgs[step][:, pl.ds(far + past, LANES)].astype(F32)
                total += jnp.concatenate([one[:half] + other[half:], one[half:]], axis=0)
            tags[:, pl.ds(tile * LANES, LANES)] = total
    sums = refs[:grp]
    data, product, parts = refs[grp:]
    label = tags[:, pl.ds(steps[0] * CORES * count, lanes)].astype(jnp.int32)
    key = label[0:1] * CPAD + label[1:2]
    spot = label[2:3]
    turn = label[3:4]
    pick = (
        lax.broadcasted_iota(jnp.int32, (PIECES * BINS, lanes), 0) % BINS == spot
    ).astype(BF16)
    klass = lax.broadcasted_iota(jnp.int32, (CPAD, lanes), 0)
    member = []
    for step in range(grp):
        one = (klass + CPAD * partner(own, step, grp) == key).astype(BF16)
        member.append(jnp.concatenate([one, one], axis=1))
    eye = identity()
    for tile in range(tiles):
        across = pl.ds(tile * LANES, LANES)
        flipped = lax.dot_general(eye, data[:, across], NT, preferred_element_type=F32)
        ctf = jnp.dot(
            pieces[pl.ds((base + tile) * LANES, LANES), :], pick, preferred_element_type=F32
        )
        product[across, :] = flipped * ctf
    offset = rows[0] * ANGLES - base * LANES

    def rotate(q, carry):
        for tile in range(lanes // LANES):
            block = product[
                pl.ds(pl.multiple_of(offset + q * ANGLES, ROWS), ANGLES),
                pl.ds(tile * LANES, LANES),
            ]
            bits = turn[:, tile * LANES : (tile + 1) * LANES]
            for level in range(LEVELS):
                chosen = (bits >> level & 1) == 1
                block = jnp.where(chosen, turned(block, SHIFT << level), block)
            high, low = split(block)
            where = pl.ds(pl.multiple_of(q * ANGLES, 2 * ROWS), ANGLES)
            parts[where, pl.ds(tile * LANES, LANES)] = high
            parts[where, pl.ds(lanes + tile * LANES, LANES)] = low
        return carry

    lax.fori_loop(0, rows[1] - rows[0], rotate, 0, unroll=True)
    result = lax.dot_general(
        jnp.concatenate(member, axis=0), parts[...], NT, preferred_element_type=F32
    )
    for step in range(grp):
        for tile, width in stacked(result.shape[1]):
            here = (pl.ds(tile * CPG, CPG), pl.ds(0, width))
            value = result[step * CPAD : step * CPAD + CPG, tile * LANES : tile * LANES + width]
            sums[step][here] = value + partial[step][here] if partial else value
        if first:
            target = partner(own, step, grp)
            local = jnp.where(label[0:1] == target, label[1:2], -1)
            row = CPG * len(stacked(result.shape[1]))
            for kind in (local, spot, turn):
                for tile in range(lanes // LANES):
                    value = kind[:, tile * LANES : (tile + 1) * LANES].astype(F32)
                    sums[step][pl.ds(row, 1), :] = value
                    row += 1


def numerators(count, pieces, tags, arrived, chunk, edges, rows, steps, partial, after):
    mem, grp = lax.axis_size("mem"), lax.axis_size("grp")
    first = chunk == 0
    here = (rows[chunk], rows[chunk + 1])
    base = here[0] * ANGLES // LANES
    stop = min(-(-here[1] * ANGLES // LANES), edges[-1])
    segments, msgs = [], []
    for c in range(chunk + 1):
        low, high = max(edges[c], base), min(edges[c + 1], stop)
        if low < high:
            segments.append((c, edges[c + 1] - edges[c], low - edges[c], low - base, high - low))
            msgs += arrived[c][slice(*steps)]
    lanes = (steps[1] - steps[0]) * CORES * count
    span = (here[1] - here[0]) * ANGLES
    tiles = stop - base
    shapes = [jax.ShapeDtypeStruct((ROWS, lanes), F32)] if first else []
    tall = sum_rows(span, lanes if first else 0)
    shapes += [jax.ShapeDtypeStruct((tall, LANES), F32)] * grp
    operands = [pieces] + ([] if first else [tags]) + msgs + list(partial)
    outs = pl.pallas_call(
        functools.partial(
            numer_kernel, mem, count, first, here, base, tiles, tuple(segments), steps, len(partial),
            len(after),
        ),
        out_shape=shapes,
        in_specs=[VMEM] * len(operands) + [ANY] * len(after),
        out_specs=[VMEM] * len(shapes),
        scratch_shapes=[
            pltpu.VMEM((lanes, tiles * LANES), BF16),
            pltpu.VMEM((tiles * LANES, lanes), F32),
            pltpu.VMEM((span, 2 * lanes), BF16),
        ],
        name="numerators",
        **params(16),
    )(*operands, *after)
    if first:
        return outs[0], outs[1:]
    return tags, outs


def denom_kernel(first, lanes, weights, *refs):
    blocks, (denom, spread) = refs[:-2], refs[-2:]
    span = weights.shape[0]
    klass = lax.broadcasted_iota(jnp.int32, (CPAD, lanes), 0)
    pair = lax.broadcasted_iota(jnp.int32, (PAIRS, lanes), 0)
    count = jnp.zeros((CPAD, PAIRS), F32)
    for ref in blocks:
        local, spot, turn = [label.astype(jnp.int32) for label in read_tags(ref, first, lanes)]
        member = (klass == local).astype(BF16)
        which = (pair == turn * BINS + spot).astype(BF16)
        count += lax.dot_general(member, which, NT, preferred_element_type=F32)
    high, low = split(count)
    left = jnp.concatenate(
        [jnp.concatenate([high, high], axis=1), jnp.concatenate([low, low], axis=1)], axis=0
    )

    def turn_far(q, carry):
        rows = pl.ds(pl.multiple_of(q * ANGLES, 2 * ROWS), ANGLES)
        block = weights[rows, :]
        for tile in range(PAIRS // LANES):
            far = turned(block, SHIFT * NEAR * tile)
            spread[rows, pl.ds(tile * LANES, LANES)] = far[:, :LANES]
            spread[rows, pl.ds(PAIRS + tile * LANES, LANES)] = far[:, LANES:]
        return carry

    lax.fori_loop(0, span // ANGLES, turn_far, 0, unroll=True)
    both = lax.dot_general(left, spread[...], NT, preferred_element_type=F32)
    denom[...] = both[:CPAD] + both[CPAD:]


def denominators(weights, blocks, first, lanes):
    span = weights.shape[0]
    return pl.pallas_call(
        functools.partial(denom_kernel, first, lanes),
        out_shape=jax.ShapeDtypeStruct((CPAD, span), F32),
        in_specs=[VMEM] * (1 + len(blocks)),
        out_specs=VMEM,
        scratch_shapes=[pltpu.VMEM((span, 2 * PAIRS), BF16)],
        name="denominators",
        **params(20),
    )(weights, *blocks)


def average_kernel(rows, denom, *refs):
    *sums, final, out, sems = refs
    copies = []
    for chunk in range(len(rows) - 1):
        for tile, width in stacked((rows[chunk + 1] - rows[chunk]) * ANGLES):
            across = pl.ds(rows[chunk] * ANGLES + tile * LANES, width)
            total = sums[chunk][pl.ds(tile * CPG, CPG), pl.ds(0, width)]
            out[:, across] = total / (denom[:CPG, across] + wiener_term)
        across = pl.ds(rows[chunk] * ANGLES, (rows[chunk + 1] - rows[chunk]) * ANGLES)
        copies.append(pltpu.make_async_copy(out.at[:, across], final.at[:, across], sems.at[chunk]))
        copies[-1].start()
    for copy in copies:
        copy.wait()


def averages(denom, sums, rows):
    span = denom.shape[1]
    return pl.pallas_call(
        functools.partial(average_kernel, rows),
        out_shape=jax.ShapeDtypeStruct((CPG, span), F32),
        in_specs=[VMEM] * (1 + len(sums)),
        out_specs=HBM,
        scratch_shapes=[
            pltpu.VMEM((CPG, span), F32),
            pltpu.SemaphoreType.DMA((len(sums),)),
        ],
        name="averages",
        **params(8),
    )(denom, *sums)


def plan(span):
    turns = span // ANGLES
    tiles = -(-span // LANES)
    edges = [0, tiles // 2, tiles] if tiles % 2 == 0 else [0, tiles]
    rows = [min(edge * LANES // ANGLES, turns) for edge in edges]
    return tuple(edges), tuple(rows)


def on_device(images, classes, rotations, bins, ctf_table):
    mem, grp = lax.axis_size("mem"), lax.axis_size("grp")
    count = images.shape[0]
    span = images.shape[1] // mem
    edges, rows = plan(span)
    cols = edges[-1] * LANES
    places = mem // CORES
    table = ctf_table
    if cols != span:
        images = jnp.pad(images.reshape(count, mem, span), ((0, 0), (0, 0), (0, cols - span)))
        images = images.reshape(count, mem * cols)
        table = lax.dynamic_slice_in_dim(ctf_table, lax.axis_index("mem") * span, span, 1)
        table = jnp.pad(table, ((0, 0), (0, cols - span)))
    pieces, weights = tables(table, cols, span // ANGLES)
    chunks = pack(images, jnp.stack([classes, bins, rotations]), cols, edges)
    arrived, after, ties = [], [], []
    for kept, crossed in chunks:
        msgs = join(kept, send(crossed, "mem", 0, CORES, 1), after)
        here = {step: send(msgs[step], "mem", step, CORES) for step in range(places - 1, 0, -1)}
        here[0] = msgs[0]
        arrived.append([here[step] for step in range(places)])
        after = [pieces]
        ties = [msgs[0]] if len(arrived) > 1 else []
    tags, sums, blocks = None, [], []
    for chunk in range(len(edges) - 1):
        cuts = [0, places]
        if chunk > 0 and places // 2 * CORES * count % LANES == 0:
            cuts = [0, places // 2, places]
        here = ()
        for steps in zip(cuts, cuts[1:]):
            tie = [] if chunk else ties
            tags, here = numerators(
                count, pieces, tags, arrived, chunk, edges, rows, steps, here, tie
            )
        others = [send(here[step].astype(HALF), "grp", step) for step in range(1, grp)]
        if chunk == 0:
            blocks = [tag_block(part, rows[1] * ANGLES) for part in [here[0]] + others]
        total = here[0]
        for part in others:
            total = total + part.astype(F32)
        sums.append(total)
    denom = denominators(weights, blocks, rows[1] * ANGLES, mem * count)
    return averages(denom, sums, rows)


def solution(mesh):
    in_specs = (
        P(("grp", "mem"), None),
        P(("grp", "mem")),
        P(("grp", "mem")),
        P(("grp", "mem")),
        P(),
    )
    out_specs = P("grp", "mem")
    return jax.shard_map(
        on_device, mesh=mesh, in_specs=in_specs, out_specs=out_specs, check_vma=False
    )
```
